1024 devices in a mesh: seq: 128 (over x, z, core), head: 8 (over y).
Axes of the slice: x: 4, y: 8, z: 16, core: 2. Of those that a mesh axis runs over, the one named last changes fastest.
Arguments:
- query: bfloat16 [16384, 2048], P('seq', 'head'), may hold values from -6 to 6
- key: bfloat16 [16384, 2048], P('seq', 'head'), may hold values from -6 to 6
- value: bfloat16 [16384, 2048], P('seq', 'head'), may hold values from -6 to 6
- gain: float32 [2048], P('head'), may hold values from 0.1 to 1.9
- grad_out: bfloat16 [16384, 2048], P('seq', 'head'), may hold values from -48 to 48
Outputs:
- grad_query: float32 [16384, 2048], P('seq', 'head')
- grad_key: float32 [16384, 2048], P('seq', 'head')
- grad_value: float32 [16384, 2048], P('seq', 'head')
The draws below stay inside these ranges and needn't reach their ends.
All inputs are finite; a program needn't handle non-finite values.
Results may differ from the reference program's by a relative error of at most 0.0003.
Values sent between devices are 32-bit elements; how exact they have to be, the bound alone decides.
No kernel may reach another device: no remote copies, remote signals or barrier semaphores. Data moves between devices by JAX's collectives and lax.ppermute only.
A program may use at most 128 MiB of HBM per device.

```python
import jax
import jax.numpy as jnp
from jax import lax

HEADS = 16
HD = 128
TOK_DEV = 128
D = 2048
TOKENS = 16384


def block_levels(own_key, extent, cuts, smallest, top_value):
    loudness, own = 1.0, jax.random.fold_in(own_key, 6)
    for dim, shards_of in cuts:
        draws = jnp.exp(jax.random.uniform(jax.random.fold_in(own, dim), (shards_of,), jnp.float32, smallest / len(cuts), top_value / len(cuts)))
        loudness = loudness * jnp.repeat(draws, extent[dim] // shards_of).reshape([-1 if axis == dim else 1 for axis in range(len(extent))])
    return loudness


def gaussian(own_key, dims, width, bound, cuts=(), dtype=jnp.bfloat16):
    entries = width * jax.random.normal(own_key, dims, jnp.float32)
    if cuts:
        entries = entries * block_levels(own_key, dims, cuts, -0.22, 0.18)
    return jnp.clip(entries, -bound, bound).astype(dtype)


def setup_inputs(seed: int = 0) -> dict:
    key_list = jax.random.split(jax.random.key(seed), 6)
    query = gaussian(key_list[0], (TOKENS, D), 1.0, 6.0, ((0, 128), (1, 8)))
    key = gaussian(key_list[1], (TOKENS, D), 1.0, 6.0, ((0, 128), (1, 8)))
    value = gaussian(key_list[2], (TOKENS, D), 1.0, 6.0, ((0, 128), (1, 8)))
    gain = jnp.clip(1.0 + 0.18 * jax.random.normal(key_list[3], (D,), jnp.float32), 0.1, 1.9)
    grad_out = gaussian(key_list[4], (TOKENS, D), 8.0, 48.0, ((0, 128), (1, 8)))
    return dict(query=query, key=key, value=value, gain=gain, grad_out=grad_out)


def feature(raw):
    wide = raw.astype(jnp.float32)
    return jnp.where(wide > 0, wide + 1.0, jnp.exp(jnp.minimum(wide, 0.0)))

def slope(raw):
    wide = raw.astype(jnp.float32)
    return jnp.where(wide > 0, 1.0, jnp.exp(jnp.minimum(wide, 0.0)))

def product(form, left, right):
    return jnp.einsum(form, left, right, precision=lax.Precision.HIGHEST, preferred_element_type=jnp.float32)

def norm_grad(output, gain_row, grad_norm):
    inverse = lax.rsqrt(lax.optimization_barrier(jnp.mean(output * output, axis=-1, keepdims=True)) + 1e-06)
    normed = output * inverse
    scaled = gain_row * grad_norm
    return inverse * (scaled - normed * lax.optimization_barrier(jnp.mean(scaled * normed, axis=-1, keepdims=True)))

def reference(query, key, value, gain, grad_out):
    total_rows = query.shape[0]
    num_blocks = total_rows // TOK_DEV

    def split(array):
        return array.astype(jnp.float32).reshape(num_blocks, TOK_DEV, HEADS, HD).transpose(0, 2, 1, 3)

    def joined(array):
        return array.transpose(0, 2, 1, 3).reshape(total_rows, HEADS * HD)
    query_all = split(query)
    key_all = split(key)
    value_all = split(value)
    grad_all = split(grad_out)
    gain_row = gain.astype(jnp.float32).reshape(HEADS, 1, HD)
    causal_mask = jnp.tril(jnp.ones((TOK_DEV, TOK_DEV), jnp.float32))
    zero_state = jnp.zeros((HEADS, HD, HD), jnp.float32)

    def forward_step(state_kv, pieces):
        query_blk, key_blk, value_blk, grad_blk = pieces
        query_feat = feature(query_blk)
        key_feat = feature(key_blk)
        scores = product('hti,hsi->hts', query_feat, key_feat) * causal_mask
        output = product('hts,hsj->htj', scores, value_blk) + product('hti,hij->htj', query_feat, state_kv)
        grad_o = norm_grad(output, gain_row, grad_blk)
        grad_scores = product('htj,hsj->hts', grad_o, value_blk) * causal_mask
        grad_q = slope(query_blk) * (product('hts,hsi->hti', grad_scores, key_feat) + product('htj,hij->hti', grad_o, state_kv))
        state_kv = state_kv + product('hsi,hsj->hij', key_feat, value_blk)
        return (state_kv, (grad_o, grad_q))
    unused, (grad_os, grad_qs) = lax.scan(forward_step, zero_state, (query_all, key_all, value_all, grad_all))

    def backward_step(state_qg, pieces):
        query_blk, key_blk, value_blk, grad_o = pieces
        query_feat = feature(query_blk)
        key_feat = feature(key_blk)
        scores = product('hti,hsi->hts', query_feat, key_feat) * causal_mask
        grad_scores = product('htj,hsj->hts', grad_o, value_blk) * causal_mask
        grad_k = slope(key_blk) * (product('hts,hti->hsi', grad_scores, query_feat) + product('hsj,hij->hsi', value_blk, state_qg))
        grad_v = product('hts,htj->hsj', scores, grad_o) + product('hsi,hij->hsj', key_feat, state_qg)
        state_qg = state_qg + product('hti,htj->hij', query_feat, grad_o)
        return (state_qg, (grad_k, grad_v))
    unused2, (grad_ks, grad_vs) = lax.scan(backward_step, zero_state, (query_all, key_all, value_all, grad_os), reverse=True)
    return (joined(grad_qs), joined(grad_ks), joined(grad_vs))
```

```python
import functools

import jax
import jax.numpy as jnp
from jax import lax
from jax.experimental import pallas as pl
from jax.experimental.pallas import tpu as pltpu
from jax.sharding import Mesh, PartitionSpec as P

HD = 128
F32 = jnp.float32
BF16 = jnp.bfloat16
VMEM = pl.BlockSpec(memory_space=pltpu.VMEM)
SMEM = pl.BlockSpec(memory_space=pltpu.SMEM)
NN = (((1,), (0,)), ((), ()))
NT = (((1,), (1,)), ((), ()))
TN = (((0,), (0,)), ((), ()))


def halves(wide):
    high = wide.astype(BF16)
    low = (wide - high.astype(F32)).astype(BF16)
    return high, low


def one(left, right, dims):
    return lax.dot_general(left, right, dims, preferred_element_type=F32)


def product(left, right, dims):
    if not isinstance(left, tuple):
        return one(left, right[0], dims) + one(left, right[1], dims)
    if not isinstance(right, tuple):
        return one(left[0], right, dims) + one(left[1], right, dims)
    return one(left[0], right[0], dims) + (one(left[0], right[1], dims) + one(left[1], right[0], dims))


def feature(raw):
    wide = raw.astype(F32)
    return jnp.where(wide > 0, wide + 1.0, jnp.exp(jnp.minimum(wide, 0.0)))


def slope(raw):
    wide = raw.astype(F32)
    return jnp.where(wide > 0, 1.0, jnp.exp(jnp.minimum(wide, 0.0)))


def causal(size):
    row = lax.broadcasted_iota(jnp.int32, (size, size), 0)
    column = lax.broadcasted_iota(jnp.int32, (size, size), 1)
    return row >= column


def columns(index):
    return pl.ds(pl.multiple_of(index * HD, HD), HD)


def pack_kernel(core_ref, q_ref, k_ref, v_ref, g_ref, out_ref):
    other = 1 - core_ref[0]
    for place, ref in enumerate((q_ref, k_ref, v_ref, g_ref)):
        out_ref[place] = ref[:, columns(other)].astype(F32)


def local_kernel(core_ref, q_ref, k_ref, v_ref, g_ref, got_ref, qo_ref, ko_ref, vo_ref, go_ref, state_ref):
    core = core_ref[0]
    other = 1 - core
    pairs = ((q_ref, qo_ref), (k_ref, ko_ref), (v_ref, vo_ref), (g_ref, go_ref))
    for place, (ref, out_ref) in enumerate(pairs):
        out_ref[columns(core), :] = ref[:, columns(core)]
        out_ref[columns(other), :] = got_ref[other, place].astype(BF16)
    state_ref[...] = product(halves(feature(ko_ref[...])), vo_ref[...], TN)


def prefix_kernel(rows, backward, pieces_ref, out_ref):
    size = pieces_ref.shape[0]
    row = lax.broadcasted_iota(jnp.int32, (size, size), 0)
    column = lax.broadcasted_iota(jnp.int32, (size, size), 1)
    same = lax.rem(row, rows) == lax.rem(column, rows)
    apart = row - column if not backward else column - row
    taken = jnp.where(same & (apart > 0), 1.0, 0.0).astype(BF16)
    out_ref[...] = product(taken, halves(pieces_ref[...]), NN)


def forward_kernel(q_ref, k_ref, v_ref, g_ref, gain_ref, prefix_ref, scores_ref, grad_ref, state_ref):
    size = q_ref.shape[0]
    query = halves(feature(q_ref[...]))
    key = halves(feature(k_ref[...]))
    scores = jnp.where(causal(size), product(query, key, NT), 0.0)
    scores_ref[...] = scores
    output = product(halves(scores), v_ref[...], NN) + product(query, halves(prefix_ref[...]), NN)
    inverse = lax.rsqrt(jnp.mean(output * output, axis=-1, keepdims=True) + 1e-06)
    normed = output * inverse
    scaled = gain_ref[...] * g_ref[...].astype(F32)
    grad = inverse * (scaled - normed * jnp.mean(scaled * normed, axis=-1, keepdims=True))
    grad_ref[...] = grad
    state_ref[...] = product(query, halves(grad), TN)


def inner_kernel(q_ref, k_ref, v_ref, scores_ref, grad_ref, prefix_ref, dq_ref, dk_ref, dv_ref):
    size = q_ref.shape[0]
    query = halves(feature(q_ref[...]))
    key = halves(feature(k_ref[...]))
    grad = halves(grad_ref[...])
    grad_scores = halves(jnp.where(causal(size), product(grad, v_ref[...], NT), 0.0))
    dq = product(grad_scores, key, NN) + product(grad, halves(prefix_ref[...]), NT)
    dq_ref[...] = slope(q_ref[...]) * dq
    dk_ref[...] = product(grad_scores, query, TN)
    dv_ref[...] = product(halves(scores_ref[...]), grad, TN)


def backward_kernel(core_ref, k_ref, v_ref, dq_ref, dk_ref, dv_ref, suffix_ref, own_ref, send_ref):
    core = core_ref[0]
    suffix = halves(suffix_ref[...])

    def finish(index, out_ref):
        rows = columns(index)
        raw = k_ref[rows, :]
        out_ref[0] = dq_ref[rows, :]
        out_ref[1] = slope(raw) * (dk_ref[rows, :] + product(v_ref[rows, :], suffix, NT))
        out_ref[2] = dv_ref[rows, :] + product(halves(feature(raw)), suffix, NN)

    finish(core, own_ref)
    finish(1 - core, send_ref)


def place_kernel(core_ref, own_ref, got_ref, dq_ref, dk_ref, dv_ref):
    core = core_ref[0]
    other = 1 - core
    for place, ref in enumerate((dq_ref, dk_ref, dv_ref)):
        ref[:, columns(core)] = own_ref[place]
        ref[:, columns(other)] = got_ref[other, place]


def call(kernel, outs, *operands, scalars=0):
    return pl.pallas_call(
        kernel,
        out_shape=[jax.ShapeDtypeStruct(shape, dtype) for shape, dtype in outs],
        in_specs=[SMEM] * scalars + [VMEM] * (len(operands) - scalars),
        out_specs=[VMEM] * len(outs),
    )(*operands)


def scan_chips(state, backward):
    chips = lax.axis_size("x") * lax.axis_size("z")
    rows = HD // chips
    pieces = lax.all_to_all(state.reshape(chips, rows, HD), ("x", "z"), 0, 0)
    kernel = functools.partial(prefix_kernel, rows, backward)
    (sums,) = call(kernel, [((HD, HD), F32)], pieces.reshape(HD, HD))
    return lax.all_to_all(sums.reshape(chips, rows, HD), ("x", "z"), 0, 0).reshape(HD, HD)


def body(query, key, value, gain, grad_out):
    tokens = query.shape[0]
    core = lax.axis_index("c")
    at = core.reshape(1)
    gain_row = lax.dynamic_slice(gain, (core * HD,), (HD,)).reshape(1, HD)
    (sent,) = call(pack_kernel, [((4, tokens, HD), F32)], at, query, key, value, grad_out, scalars=1)
    got = lax.all_gather(sent, "c")
    pair = (2 * tokens, HD)
    q, k, v, g, state = call(
        local_kernel,
        [(pair, BF16)] * 4 + [((HD, HD), F32)],
        at, query, key, value, grad_out, got,
        scalars=1,
    )
    prefix = scan_chips(state, False)
    scores, grad, state = call(
        forward_kernel,
        [((2 * tokens, 2 * tokens), F32), (pair, F32), ((HD, HD), F32)],
        q, k, v, g, gain_row, prefix,
    )
    suffix = scan_chips(state, True)
    dq, dk, dv = call(inner_kernel, [(pair, F32)] * 3, q, k, v, scores, grad, prefix)
    own, send = call(backward_kernel, [((3, tokens, HD), F32)] * 2, at, k, v, dq, dk, dv, suffix, scalars=1)
    got = lax.all_gather(send, "c")
    return tuple(call(place_kernel, [((tokens, 2 * HD), F32)] * 3, at, own, got, scalars=1))


def over(devices):
    mesh = Mesh(devices, ("x", "z", "c", "h"))
    placed = P(("x", "z", "c"), "h")
    return jax.shard_map(
        body,
        mesh=mesh,
        in_specs=(placed, placed, placed, P("h"), placed),
        out_specs=(placed, placed, placed),
        check_vma=False,
    )


def solution(mesh):
    seq, head = mesh.devices.shape
    return over(mesh.devices.reshape(4, seq // 8, 2, head))
```

```python
import functools

import jax
import jax.numpy as jnp
from jax import lax
from jax.experimental import pallas as pl
from jax.experimental.pallas import tpu as pltpu
from jax.sharding import Mesh, PartitionSpec as P

HD = 128
F32 = jnp.float32
BF16 = jnp.bfloat16
VMEM = pl.BlockSpec(memory_space=pltpu.VMEM)
SMEM = pl.BlockSpec(memory_space=pltpu.SMEM)
NN = (((1,), (0,)), ((), ()))
NT = (((1,), (1,)), ((), ()))
TN = (((0,), (0,)), ((), ()))


def halves(wide):
    high = wide.astype(BF16)
    low = (wide - high.astype(F32)).astype(BF16)
    return high, low


def one(left, right, dims):
    return lax.dot_general(left, right, dims, preferred_element_type=F32)


def product(left, right, dims):
    if not isinstance(left, tuple):
        return one(left, right[0], dims) + one(left, right[1], dims)
    if not isinstance(right, tuple):
        return one(left[0], right, dims) + one(left[1], right, dims)
    return one(left[0], right[0], dims) + (one(left[0], right[1], dims) + one(left[1], right[0], dims))


def feature(raw):
    wide = raw.astype(F32)
    return jnp.where(wide > 0, wide + 1.0, jnp.exp(jnp.minimum(wide, 0.0)))


def slope(raw):
    wide = raw.astype(F32)
    return jnp.where(wide > 0, 1.0, jnp.exp(jnp.minimum(wide, 0.0)))


def causal(size):
    row = lax.broadcasted_iota(jnp.int32, (size, size), 0)
    column = lax.broadcasted_iota(jnp.int32, (size, size), 1)
    return row >= column


def columns(index):
    return pl.ds(pl.multiple_of(index * HD, HD), HD)


def pack_kernel(core_ref, q_ref, k_ref, v_ref, g_ref, send_ref, own_ref, other_ref, sems):
    core = core_ref[0]
    copies = []
    for part, (head, into) in enumerate(((1 - core, other_ref), (core, own_ref))):
        for place, ref in enumerate((q_ref, k_ref, v_ref, g_ref)):
            copy = pltpu.make_async_copy(ref.at[:, columns(head)], into.at[place], sems.at[4 * part + place])
            copy.start()
            copies.append(copy)
    for place in range(4):
        copies[place].wait()
        send_ref[place] = other_ref[place].astype(F32)
    for copy in copies[4:]:
        copy.wait()


def local_kernel(core_ref, own_ref, got_ref, qo_ref, ko_ref, vo_ref, go_ref, state_ref):
    core = core_ref[0]
    other = 1 - core
    for place, out_ref in enumerate((qo_ref, ko_ref, vo_ref, go_ref)):
        out_ref[columns(core), :] = own_ref[place]
        out_ref[columns(other), :] = got_ref[other, place].astype(BF16)
    state_ref[...] = product(halves(feature(ko_ref[...])), vo_ref[...], TN)


def prefix_kernel(rows, backward, pieces_ref, out_ref):
    size = pieces_ref.shape[0]
    row = lax.broadcasted_iota(jnp.int32, (size, size), 0)
    column = lax.broadcasted_iota(jnp.int32, (size, size), 1)
    same = lax.rem(row, rows) == lax.rem(column, rows)
    apart = row - column if not backward else column - row
    taken = jnp.where(same & (apart > 0), 1.0, 0.0).astype(BF16)
    out_ref[...] = product(taken, halves(pieces_ref[...]), NN)


def scores_kernel(q_ref, k_ref, v_ref, scores_ref, near_ref):
    query = halves(feature(q_ref[...]))
    key = halves(feature(k_ref[...]))
    scores = jnp.where(causal(q_ref.shape[0]), product(query, key, NT), 0.0)
    scores_ref[...] = scores
    near_ref[...] = product(halves(scores), v_ref[...], NN)


def forward_kernel(q_ref, g_ref, gain_ref, near_ref, prefix_ref, grad_ref, state_ref):
    query = halves(feature(q_ref[...]))
    output = near_ref[...] + product(query, halves(prefix_ref[...]), NN)
    inverse = lax.rsqrt(jnp.mean(output * output, axis=-1, keepdims=True) + 1e-06)
    normed = output * inverse
    scaled = gain_ref[...] * g_ref[...].astype(F32)
    grad = inverse * (scaled - normed * jnp.mean(scaled * normed, axis=-1, keepdims=True))
    grad_ref[...] = grad
    state_ref[...] = product(query, halves(grad), TN)


def inner_kernel(core_ref, q_ref, k_ref, v_ref, scores_ref, grad_ref, prefix_ref, own_ref, send_ref, all_ref):
    core = core_ref[0]
    query = halves(feature(q_ref[...]))
    key = halves(feature(k_ref[...]))
    grad = halves(grad_ref[...])
    grad_scores = halves(jnp.where(causal(q_ref.shape[0]), product(grad, v_ref[...], NT), 0.0))
    dq = product(grad_scores, key, NN) + product(grad, halves(prefix_ref[...]), NT)
    all_ref[0] = slope(q_ref[...]) * dq
    all_ref[1] = product(grad_scores, query, TN)
    all_ref[2] = product(halves(scores_ref[...]), grad, TN)
    for place in range(3):
        own_ref[place] = all_ref[place, columns(core), :]
        send_ref[place] = all_ref[place, columns(1 - core), :]


def place_kernel(core_ref, own_ref, got_ref, dq_ref, dk_ref, dv_ref):
    core = core_ref[0]
    other = 1 - core
    for place, ref in enumerate((dq_ref, dk_ref, dv_ref)):
        ref[:, columns(core)] = own_ref[place]
        ref[:, columns(other)] = got_ref[other, place]


def backward_kernel(k_ref, v_ref, near_dk_ref, near_dv_ref, suffix_ref, dk_ref, dv_ref):
    for head in range(2):
        part = slice(head * HD, head * HD + HD)
        suffix = halves(suffix_ref[head])
        raw = k_ref[:, part]
        dk_ref[:, part] = slope(raw) * (near_dk_ref[:, part] + product(v_ref[:, part], suffix, NT))
        dv_ref[:, part] = near_dv_ref[:, part] + product(halves(feature(raw)), suffix, NN)


def call(kernel, outs, *operands, scalars=0, space=pltpu.VMEM, scratch=()):
    others = [pl.BlockSpec(memory_space=space)] * (len(operands) - scalars)
    return pl.pallas_call(
        kernel,
        out_shape=[jax.ShapeDtypeStruct(shape, dtype) for shape, dtype in outs],
        in_specs=[SMEM] * scalars + others,
        out_specs=[VMEM] * len(outs),
        scratch_shapes=scratch,
        compiler_params=pltpu.CompilerParams(vmem_limit_bytes=8 << 20),
    )(*operands)


def scan_chips(state, backward):
    chips = lax.axis_size("x") * lax.axis_size("z")
    rows = HD // chips
    pieces = lax.all_to_all(state.reshape(chips, rows, HD), ("x", "z"), 0, 0)
    kernel = functools.partial(prefix_kernel, rows, backward)
    (sums,) = call(kernel, [((HD, HD), F32)], pieces.reshape(HD, HD))
    return lax.all_to_all(sums.reshape(chips, rows, HD), ("x", "z"), 0, 0).reshape(HD, HD)


def body(query, key, value, gain, grad_out):
    tokens = query.shape[0]
    core = lax.axis_index("c")
    at = core.reshape(1)
    gain_row = lax.dynamic_slice(gain, (core * HD,), (HD,)).reshape(1, HD)
    four, three, pair, state_shape = (4, tokens, HD), (3, tokens, HD), (2 * tokens, HD), (HD, HD)
    send, own = call(
        pack_kernel,
        [(four, F32), (four, BF16)],
        at, *(pltpu.with_memory_space_constraint(array, pltpu.HBM) for array in (query, key, value, grad_out)),
        scalars=1, space=pltpu.HBM, scratch=[pltpu.VMEM(four, BF16), pltpu.SemaphoreType.DMA((8,))],
    )
    got = lax.all_gather(send, "c")
    q, k, v, g, state = call(local_kernel, [(pair, BF16)] * 4 + [(state_shape, F32)], at, own, got, scalars=1)
    prefix = scan_chips(state, False)
    scores, near = call(scores_kernel, [((2 * tokens, 2 * tokens), F32), (pair, F32)], q, k, v)
    grad, state = call(forward_kernel, [(pair, F32), (state_shape, F32)], q, g, gain_row, near, prefix)
    suffix = scan_chips(state, True)
    own, send = call(
        inner_kernel,
        [(three, F32)] * 2,
        at, q, k, v, scores, grad, prefix,
        scalars=1, scratch=[pltpu.VMEM((3,) + pair, F32)],
    )
    got = lax.all_gather(send, "c")
    whole = ((tokens, 2 * HD), F32)
    dq, dk, dv = call(place_kernel, [whole] * 3, at, own, got, scalars=1)
    dk, dv = call(backward_kernel, [whole] * 2, key, value, dk, dv, lax.all_gather(suffix, "c"))
    return dq, dk, dv


def over(devices):
    mesh = Mesh(devices, ("x", "z", "c", "h"))
    placed = P(("x", "z", "c"), "h")
    return jax.shard_map(
        body,
        mesh=mesh,
        in_specs=(placed, placed, placed, P("h"), placed),
        out_specs=(placed, placed, placed),
        check_vma=False,
    )


def solution(mesh):
    seq, head = mesh.devices.shape
    return over(mesh.devices.reshape(4, seq // 8, 2, head))
```

```python
import functools

import jax
import jax.numpy as jnp
from jax import lax
from jax.experimental import pallas as pl
from jax.experimental.pallas import tpu as pltpu
from jax.sharding import Mesh, PartitionSpec as P

HD = 128
F32 = jnp.float32
BF16 = jnp.bfloat16
VMEM = pl.BlockSpec(memory_space=pltpu.VMEM)
SMEM = pl.BlockSpec(memory_space=pltpu.SMEM)
NN = (((1,), (0,)), ((), ()))
NT = (((1,), (1,)), ((), ()))
TN = (((0,), (0,)), ((), ()))


def halves(wide):
    high = wide.astype(BF16)
    low = (wide - high.astype(F32)).astype(BF16)
    return high, low


def one(left, right, dims):
    return lax.dot_general(left, right, dims, preferred_element_type=F32)


def product(left, right, dims):
    if not isinstance(left, tuple):
        return one(left, right[0], dims) + one(left, right[1], dims)
    if not isinstance(right, tuple):
        return one(left[0], right, dims) + one(left[1], right, dims)
    return one(left[0], right[0], dims) + (one(left[0], right[1], dims) + one(left[1], right[0], dims))


def feature(raw):
    wide = raw.astype(F32)
    return jnp.where(wide > 0, wide + 1.0, jnp.exp(jnp.minimum(wide, 0.0)))


def slope(raw):
    wide = raw.astype(F32)
    return jnp.where(wide > 0, 1.0, jnp.exp(jnp.minimum(wide, 0.0)))


def causal(size):
    row = lax.broadcasted_iota(jnp.int32, (size, size), 0)
    column = lax.broadcasted_iota(jnp.int32, (size, size), 1)
    return row >= column


def columns(index):
    return pl.ds(pl.multiple_of(index * HD, HD), HD)


def core_of(at_ref):
    return lax.rem(at_ref[0], 2)


def pack_kernel(at_ref, q_ref, k_ref, v_ref, g_ref, gain_ref, send_ref, own_ref, gain_out_ref, other_ref, sems):
    core = core_of(at_ref)
    copies = []
    for part, (head, into) in enumerate(((1 - core, other_ref), (core, own_ref))):
        for place, ref in enumerate((q_ref, k_ref, v_ref, g_ref)):
            copy = pltpu.make_async_copy(ref.at[:, columns(head)], into.at[place], sems.at[4 * part + place])
            copy.start()
            copies.append(copy)
    copies.append(pltpu.make_async_copy(gain_ref, gain_out_ref, sems.at[8]))
    copies[8].start()
    for place in range(4):
        copies[place].wait()
        send_ref[place] = other_ref[place].astype(F32)
    for copy in copies[4:]:
        copy.wait()


def local_kernel(at_ref, own_ref, got_ref, gain_ref, qo_ref, ko_ref, vo_ref, scaled_ref, state_ref):
    core = core_of(at_ref)
    other = 1 - core
    gain_row = gain_ref[pl.ds(core, 1), :]
    for place, out_ref in enumerate((qo_ref, ko_ref, vo_ref)):
        out_ref[columns(core), :] = own_ref[place]
        out_ref[columns(other), :] = got_ref[other, place].astype(BF16)
    scaled_ref[columns(core), :] = gain_row * own_ref[3].astype(F32)
    scaled_ref[columns(other), :] = gain_row * got_ref[other, 3]
    state_ref[...] = product(halves(feature(ko_ref[...])), vo_ref[...], TN)


def total_kernel(pieces_ref, out_ref):
    total = pieces_ref[:, 0]
    for place in range(1, pieces_ref.shape[1]):
        total = total + pieces_ref[:, place]
    for block in range(out_ref.shape[0]):
        out_ref[block] = total


def prefix_kernel(backward, at_ref, pieces_ref, totals_ref, out_ref):
    x_size, place_size = pieces_ref.shape[:2]
    blocks = totals_ref.shape[0]
    block = lax.rem(lax.div(at_ref[0], 2 * place_size), blocks)
    base = jnp.zeros(pieces_ref.shape[2:], F32)
    for x in range(x_size)[:: -1 if backward else 1]:
        so_far, row = base, jnp.zeros_like(base)
        for other in range(blocks):
            total = totals_ref[other, x]
            row = row + total
            so_far = so_far + jnp.where(other > block if backward else other < block, total, 0.0)
        for place in range(place_size)[:: -1 if backward else 1]:
            out_ref[x, place] = so_far
            so_far = so_far + pieces_ref[x, place]
        base = base + row


def scores_kernel(q_ref, k_ref, v_ref, scores_ref, near_ref):
    query = halves(feature(q_ref[...]))
    key = halves(feature(k_ref[...]))
    scores = jnp.where(causal(q_ref.shape[0]), product(query, key, NT), 0.0)
    scores_ref[...] = scores
    near_ref[...] = product(halves(scores), v_ref[...], NN)


def forward_kernel(q_ref, scaled_ref, near_ref, prefix_ref, grad_ref, state_ref):
    query = halves(feature(q_ref[...]))
    output = near_ref[...] + product(query, halves(prefix_ref[...]), NN)
    inverse = lax.rsqrt(jnp.mean(output * output, axis=-1, keepdims=True) + 1e-06)
    normed = output * inverse
    scaled = scaled_ref[...]
    grad = inverse * (scaled - normed * jnp.mean(scaled * normed, axis=-1, keepdims=True))
    grad_ref[...] = grad
    state_ref[...] = product(query, halves(grad), TN)


def inner_kernel(at_ref, q_ref, k_ref, v_ref, scores_ref, grad_ref, prefix_ref, own_ref, send_ref, all_ref):
    core = core_of(at_ref)
    query = halves(feature(q_ref[...]))
    key = halves(feature(k_ref[...]))
    grad = halves(grad_ref[...])
    grad_scores = halves(jnp.where(causal(q_ref.shape[0]), product(grad, v_ref[...], NT), 0.0))
    dq = product(grad_scores, key, NN) + product(grad, halves(prefix_ref[...]), NT)
    all_ref[0] = slope(q_ref[...]) * dq
    all_ref[1] = product(grad_scores, query, TN)
    all_ref[2] = product(halves(scores_ref[...]), grad, TN)
    for place in range(3):
        own_ref[place] = all_ref[place, columns(core), :]
        send_ref[place] = all_ref[place, columns(1 - core), :]


def place_kernel(at_ref, own_ref, got_ref, dq_ref, dk_ref, dv_ref):
    core = core_of(at_ref)
    other = 1 - core
    for place, ref in enumerate((dq_ref, dk_ref, dv_ref)):
        ref[:, columns(core)] = own_ref[place]
        ref[:, columns(other)] = got_ref[other, place]


def backward_kernel(k_ref, v_ref, near_dk_ref, near_dv_ref, suffix_ref, dk_ref, dv_ref):
    for head in range(2):
        part = slice(head * HD, head * HD + HD)
        suffix = halves(suffix_ref[head])
        raw = k_ref[:, part]
        dk_ref[:, part] = slope(raw) * (near_dk_ref[:, part] + product(v_ref[:, part], suffix, NT))
        dv_ref[:, part] = near_dv_ref[:, part] + product(halves(feature(raw)), suffix, NN)


def call(kernel, outs, *operands, scalars=0, space=pltpu.VMEM, scratch=()):
    others = [pl.BlockSpec(memory_space=space)] * (len(operands) - scalars)
    return pl.pallas_call(
        kernel,
        out_shape=[jax.ShapeDtypeStruct(shape, dtype) for shape, dtype in outs],
        in_specs=[SMEM] * scalars + others,
        out_specs=[VMEM] * len(outs),
        scratch_shapes=scratch,
        compiler_params=pltpu.CompilerParams(vmem_limit_bytes=8 << 20),
    )(*operands)


def scan_chips(at, state, backward):
    blocks, x_size, place_size = lax.axis_size("zb"), lax.axis_size("x"), lax.axis_size("zp")
    members = x_size * place_size
    piece = (HD // members, HD)
    near = (x_size, place_size) + piece
    pieces = lax.all_to_all(state.reshape((members,) + piece), ("x", "zp"), 0, 0).reshape(near)
    far = (blocks, x_size) + piece
    (totals,) = call(total_kernel, [(far, F32)], pieces)
    totals = lax.all_to_all(totals, "zb", 0, 0)
    (sums,) = call(functools.partial(prefix_kernel, backward), [(near, F32)], at, pieces, totals, scalars=1)
    return lax.all_to_all(sums.reshape((members,) + piece), ("x", "zp"), 0, 0).reshape(HD, HD)


def body(query, key, value, gain, grad_out):
    tokens = query.shape[0]
    at = lax.axis_index(("x", "zb", "zp", "c")).reshape(1)
    four, three, pair, state_shape = (4, tokens, HD), (3, tokens, HD), (2 * tokens, HD), (HD, HD)
    send, own, gain = call(
        pack_kernel,
        [(four, F32), (four, BF16), ((2, HD), F32)],
        at, *(pltpu.with_memory_space_constraint(array, pltpu.HBM) for array in (query, key, value, grad_out, gain.reshape(2, HD))),
        scalars=1, space=pltpu.HBM, scratch=[pltpu.VMEM(four, BF16), pltpu.SemaphoreType.DMA((9,))],
    )
    got = lax.all_gather(send, "c")
    outs = [(pair, BF16)] * 3 + [(pair, F32), (state_shape, F32)]
    q, k, v, scaled, state = call(local_kernel, outs, at, own, got, gain, scalars=1)
    prefix = scan_chips(at, state, False)
    scores, near = call(scores_kernel, [((2 * tokens, 2 * tokens), F32), (pair, F32)], q, k, v)
    grad, state = call(forward_kernel, [(pair, F32), (state_shape, F32)], q, scaled, near, prefix)
    suffix = scan_chips(at, state, True)
    own, send = call(
        inner_kernel,
        [(three, F32)] * 2,
        at, q, k, v, scores, grad, prefix,
        scalars=1, scratch=[pltpu.VMEM((3,) + pair, F32)],
    )
    got = lax.all_gather(send, "c")
    whole = ((tokens, 2 * HD), F32)
    dq, dk, dv = call(place_kernel, [whole] * 3, at, own, got, scalars=1)
    dk, dv = call(backward_kernel, [whole] * 2, key, value, dk, dv, lax.all_gather(suffix, "c"))
    return dq, dk, dv


def over(devices):
    mesh = Mesh(devices, ("x", "zb", "zp", "c", "h"))
    placed = P(("x", "zb", "zp", "c"), "h")
    return jax.shard_map(
        body,
        mesh=mesh,
        in_specs=(placed, placed, placed, P("h"), placed),
        out_specs=(placed, placed, placed),
        check_vma=False,
    )


def solution(mesh):
    seq, head = mesh.devices.shape
    return over(mesh.devices.reshape(4, 4, seq // 32, 2, head))
```

```python
import functools

import jax
import jax.numpy as jnp
from jax import lax
from jax.experimental import pallas as pl
from jax.experimental.pallas import tpu as pltpu
from jax.sharding import Mesh, PartitionSpec as P

HD = 128
HEADS = 2
F32 = jnp.float32
BF16 = jnp.bfloat16
VMEM = pl.BlockSpec(memory_space=pltpu.VMEM)
SMEM = pl.BlockSpec(memory_space=pltpu.SMEM)
HBM = pl.BlockSpec(memory_space=pltpu.HBM)
NN = (((1,), (0,)), ((), ()))
NT = (((1,), (1,)), ((), ()))
TN = (((0,), (0,)), ((), ()))
NEAR = ("x", "zp", "c")


def halves(wide):
    high = wide.astype(BF16)
    low = (wide - high.astype(F32)).astype(BF16)
    return high, low


def one(left, right, dims):
    return lax.dot_general(left, right, dims, preferred_element_type=F32)


def product(left, right, dims):
    if not isinstance(left, tuple):
        return one(left, right[0], dims) + one(left, right[1], dims)
    if not isinstance(right, tuple):
        return one(left[0], right, dims) + one(left[1], right, dims)
    return one(left[0], right[0], dims) + (one(left[0], right[1], dims) + one(left[1], right[0], dims))


def feature(raw):
    wide = raw.astype(F32)
    return jnp.where(wide > 0, wide + 1.0, jnp.exp(jnp.minimum(wide, 0.0)))


def slope(raw):
    wide = raw.astype(F32)
    return jnp.where(wide > 0, 1.0, jnp.exp(jnp.minimum(wide, 0.0)))


def causal(size):
    row = lax.broadcasted_iota(jnp.int32, (size, size), 0)
    column = lax.broadcasted_iota(jnp.int32, (size, size), 1)
    return row >= column


def features_of(head):
    return slice(head * HD, head * HD + HD)


def local_kernel(block_ref, k_in, v_in, q_in, g_in, gain_in, k_ref, v_ref, q_ref, g_ref, gain_ref, state_ref, sems):
    pairs = ((k_in, k_ref), (v_in, v_ref), (q_in, q_ref), (g_in, g_ref), (gain_in, gain_ref))
    copies = [pltpu.make_async_copy(start, end, sems.at[place]) for place, (start, end) in enumerate(pairs)]
    for copy in copies:
        copy.start()
    copies[0].wait()
    copies[1].wait()
    for head in range(HEADS):
        part = features_of(head)
        state_ref[head] = product(halves(feature(k_ref[:, part])), v_ref[:, part], TN)
    for copy in copies[2:]:
        copy.wait()


def total_kernel(pieces_ref, out_ref):
    total = pieces_ref[:, 0]
    for place in range(1, pieces_ref.shape[1]):
        total = total + pieces_ref[:, place]
    for block in range(out_ref.shape[0]):
        out_ref[block] = total


def prefix_kernel(backward, block_ref, pieces_ref, totals_ref, out_ref):
    x_size, place_size = pieces_ref.shape[:2]
    block = block_ref[0]
    base = jnp.zeros(pieces_ref.shape[2:], F32)
    for x in range(x_size)[:: -1 if backward else 1]:
        so_far, row = base, jnp.zeros_like(base)
        for other in range(totals_ref.shape[0]):
            total = totals_ref[other, x]
            row = row + total
            so_far = so_far + jnp.where(other > block if backward else other < block, total, 0.0)
        for place in range(place_size)[:: -1 if backward else 1]:
            out_ref[x, place] = so_far
            so_far = so_far + pieces_ref[x, place]
        base = base + row


def forward_kernel(q_ref, k_ref, v_ref, g_ref, gain_ref, prefix_ref, scores_ref, grad_ref, state_ref):
    mask = causal(q_ref.shape[0])
    for head in range(HEADS):
        part = features_of(head)
        query = halves(feature(q_ref[:, part]))
        key = halves(feature(k_ref[:, part]))
        scores = jnp.where(mask, product(query, key, NT), 0.0)
        scores_ref[head] = scores
        output = product(halves(scores), v_ref[:, part], NN) + product(query, halves(prefix_ref[head]), NN)
        inverse = lax.rsqrt(jnp.mean(output * output, axis=-1, keepdims=True) + 1e-06)
        normed = output * inverse
        scaled = gain_ref[head : head + 1, :] * g_ref[:, part].astype(F32)
        grad = inverse * (scaled - normed * jnp.mean(scaled * normed, axis=-1, keepdims=True))
        grad_ref[head] = grad
        state_ref[head] = product(query, halves(grad), TN)


def backward_kernel(
    q_ref, k_ref, v_ref, scores_ref, grad_ref, prefix_ref, suffix_ref, dq_out, dk_out, dv_out, dq_ref, dk_ref, dv_ref, sems
):
    mask = causal(q_ref.shape[0])
    copies = []

    def write(start, end):
        copies.append(pltpu.make_async_copy(start, end, sems.at[len(copies)]))
        copies[-1].start()

    grads = [halves(grad_ref[head]) for head in range(HEADS)]
    keys = [halves(feature(k_ref[:, features_of(head)])) for head in range(HEADS)]
    suffixes = [halves(suffix_ref[head]) for head in range(HEADS)]
    grad_scores = []
    for head in range(HEADS):
        part = features_of(head)
        grad_scores.append(halves(jnp.where(mask, product(grads[head], v_ref[:, part], NT), 0.0)))
        dq = product(grad_scores[head], keys[head], NN) + product(grads[head], halves(prefix_ref[head]), NT)
        dq_ref[:, part] = slope(q_ref[:, part]) * dq
    write(dq_ref, dq_out)
    for head in range(HEADS):
        part = features_of(head)
        query = halves(feature(q_ref[:, part]))
        dk = product(grad_scores[head], query, TN) + product(v_ref[:, part], suffixes[head], NT)
        dk_ref[:, part] = slope(k_ref[:, part]) * dk
    write(dk_ref, dk_out)
    for head in range(HEADS):
        part = features_of(head)
        dv = product(halves(scores_ref[head]), grads[head], TN) + product(keys[head], suffixes[head], NN)
        dv_ref[:, part] = dv
    write(dv_ref, dv_out)
    for copy in copies:
        copy.wait()


def call(kernel, outs, *operands, scalars=0, inputs=VMEM, outputs=VMEM, scratch=()):
    return pl.pallas_call(
        kernel,
        out_shape=[jax.ShapeDtypeStruct(shape, dtype) for shape, dtype in outs],
        in_specs=[SMEM] * scalars + [inputs] * (len(operands) - scalars),
        out_specs=[outputs] * len(outs),
        scratch_shapes=scratch,
        compiler_params=pltpu.CompilerParams(vmem_limit_bytes=8 << 20),
    )(*operands)


def scan_devices(block, states, backward):
    blocks, x_size, members = lax.axis_size("zb"), lax.axis_size("x"), lax.axis_size(NEAR)
    piece = (HEADS * HD // members, HD)
    flat, near, far = (members,) + piece, (x_size, members // x_size) + piece, (blocks, x_size) + piece
    pieces = lax.all_to_all(states.reshape(flat), NEAR, 0, 0).reshape(near)
    (totals,) = call(total_kernel, [(far, F32)], pieces)
    totals = lax.all_to_all(totals, "zb", 0, 0)
    (sums,) = call(functools.partial(prefix_kernel, backward), [(near, F32)], block, pieces, totals, scalars=1)
    return lax.all_to_all(sums.reshape(flat), NEAR, 0, 0).reshape(HEADS, HD, HD)


def body(query, key, value, gain, grad_out):
    tokens = query.shape[0]
    block = lax.axis_index("zb").reshape(1)
    wide, per_head, state = (tokens, HEADS * HD), (HEADS, tokens, HD), ((HEADS, HD, HD), F32)
    given = (key, value, query, grad_out, gain.reshape(HEADS, HD))
    k, v, q, g, gain, states = call(
        local_kernel,
        [(wide, BF16)] * 4 + [((HEADS, HD), F32), state],
        block,
        *(pltpu.with_memory_space_constraint(array, pltpu.HBM) for array in given),
        scalars=1,
        inputs=HBM,
        scratch=[pltpu.SemaphoreType.DMA((5,))],
    )
    prefix = scan_devices(block, states, False)
    scores, grad, states = call(
        forward_kernel, [((HEADS, tokens, tokens), F32), (per_head, F32), state], q, k, v, g, gain, prefix
    )
    suffix = scan_devices(block, states, True)
    return tuple(
        call(
            backward_kernel,
            [(wide, F32)] * 3,
            *(q, k, v, scores, grad, prefix, suffix),
            outputs=HBM,
            scratch=[pltpu.VMEM(wide, F32)] * 3 + [pltpu.SemaphoreType.DMA((3,))],
        )
    )


def over(devices):
    mesh = Mesh(devices, ("x", "zb", "zp", "c", "h"))
    placed = P(("x", "zb", "zp", "c"), "h")
    return jax.shard_map(
        body,
        mesh=mesh,
        in_specs=(placed, placed, placed, P("h"), placed),
        out_specs=(placed, placed, placed),
        check_vma=False,
    )


def solution(mesh):
    seq, head = mesh.devices.shape
    return over(mesh.devices.reshape(4, 4, seq // 32, 2, head))
```

```python
import functools

import jax
import jax.numpy as jnp
from jax import lax
from jax.experimental import pallas as pl
from jax.experimental.pallas import tpu as pltpu
from jax.sharding import Mesh, PartitionSpec as P

HD = 128
HEADS = 2
F32 = jnp.float32
BF16 = jnp.bfloat16
VMEM = pl.BlockSpec(memory_space=pltpu.VMEM)
SMEM = pl.BlockSpec(memory_space=pltpu.SMEM)
HBM = pl.BlockSpec(memory_space=pltpu.HBM)
NN = (((1,), (0,)), ((), ()))
NT = (((1,), (1,)), ((), ()))
TN = (((0,), (0,)), ((), ()))
NEAR = ("x", "zp")


def halves(wide):
    high = wide.astype(BF16)
    low = (wide - high.astype(F32)).astype(BF16)
    return high, low


def one(left, right, dims):
    return lax.dot_general(left, right, dims, preferred_element_type=F32)


def product(left, right, dims):
    if not isinstance(left, tuple):
        return one(left, right[0], dims) + one(left, right[1], dims)
    if not isinstance(right, tuple):
        return one(left[0], right, dims) + one(left[1], right, dims)
    return one(left[0], right[0], dims) + (one(left[0], right[1], dims) + one(left[1], right[0], dims))


def feature(raw):
    wide = raw.astype(F32)
    return jnp.where(wide > 0, wide + 1.0, jnp.exp(jnp.minimum(wide, 0.0)))


def slope(raw):
    wide = raw.astype(F32)
    return jnp.where(wide > 0, 1.0, jnp.exp(jnp.minimum(wide, 0.0)))


def causal(size):
    row = lax.broadcasted_iota(jnp.int32, (size, size), 0)
    column = lax.broadcasted_iota(jnp.int32, (size, size), 1)
    return row >= column


def features_of(head):
    return slice(head * HD, head * HD + HD)


def local_kernel(at_ref, k_in, v_in, q_in, g_in, gain_in, k_ref, v_ref, q_ref, g_ref, gain_ref, state_ref, sems):
    pairs = ((k_in, k_ref), (v_in, v_ref), (q_in, q_ref), (g_in, g_ref), (gain_in, gain_ref))
    copies = [pltpu.make_async_copy(start, end, sems.at[place]) for place, (start, end) in enumerate(pairs)]
    for copy in copies:
        copy.start()
    copies[0].wait()
    copies[1].wait()
    for head in range(HEADS):
        part = features_of(head)
        state_ref[head] = product(halves(feature(k_ref[:, part])), v_ref[:, part], TN)
    for copy in copies[2:]:
        copy.wait()


def core_of(at_ref):
    return lax.rem(at_ref[0], 2)


def total_kernel(pieces_ref, copy_ref, out_ref):
    copy_ref[...] = pieces_ref[...]
    total = pieces_ref[:, 0]
    for place in range(1, pieces_ref.shape[1]):
        total = total + pieces_ref[:, place]
    out_ref[...] = total


def prefix_kernel(backward, steps, at_ref, pieces_ref, *refs):
    far_refs, out_ref = refs[:-1], refs[-1]
    pieces_ref = pieces_ref.at[1]
    x_size, place_size = pieces_ref.shape[:2]
    blocks = len(steps) + 1
    block = lax.rem(lax.div(at_ref[0], 2 * place_size), blocks)
    base = jnp.zeros(pieces_ref.shape[2:], F32)
    for x in range(x_size)[:: -1 if backward else 1]:
        so_far = row = base
        for step, far_ref in zip(steps, far_refs):
            other = lax.rem(block + blocks - step, blocks)
            total = far_ref[x]
            row = row + total
            so_far = so_far + jnp.where(other > block if backward else other < block, total, 0.0)
        for place in range(place_size)[:: -1 if backward else 1]:
            out_ref[x, place] = so_far
            so_far = so_far + pieces_ref[x, place]
            row = row + pieces_ref[x, place]
        base = row


def with_core(at_ref, sums_ref, states_ref, head, backward):
    first, second = (1, 0) if backward else (0, 1)
    return sums_ref[0, head] + jnp.where(core_of(at_ref) == second, states_ref[first, head], 0.0)


def forward_kernel(at_ref, q_ref, k_ref, v_ref, g_ref, gain_ref, sums_ref, states_ref, scores_ref, grad_ref, prefix_ref, state_ref):
    mask = causal(q_ref.shape[0])
    for head in range(HEADS):
        part = features_of(head)
        query = halves(feature(q_ref[:, part]))
        key = halves(feature(k_ref[:, part]))
        scores = jnp.where(mask, product(query, key, NT), 0.0)
        scores_ref[head] = scores
        prefix = with_core(at_ref, sums_ref, states_ref, head, False)
        prefix_ref[head] = prefix
        output = product(halves(scores), v_ref[:, part], NN) + product(query, halves(prefix), NN)
        inverse = lax.rsqrt(jnp.mean(output * output, axis=-1, keepdims=True) + 1e-06)
        normed = output * inverse
        scaled = gain_ref[head : head + 1, :] * g_ref[:, part].astype(F32)
        grad = inverse * (scaled - normed * jnp.mean(scaled * normed, axis=-1, keepdims=True))
        grad_ref[head] = grad
        state_ref[head] = product(query, halves(grad), TN)


def backward_kernel(at_ref, *refs):
    q_ref, k_ref, v_ref, scores_ref, grad_ref, prefix_ref, sums_ref, states_ref = refs[:8]
    dq_out, dk_out, dv_out, dq_ref, dk_ref, dv_ref, sems = refs[8:]
    mask = causal(q_ref.shape[0])
    copies = []

    def write(start, end):
        copies.append(pltpu.make_async_copy(start, end, sems.at[len(copies)]))
        copies[-1].start()

    grads = [halves(grad_ref[head]) for head in range(HEADS)]
    keys = [halves(feature(k_ref[:, features_of(head)])) for head in range(HEADS)]
    suffixes = [halves(with_core(at_ref, sums_ref, states_ref, head, True)) for head in range(HEADS)]
    grad_scores = []
    for head in range(HEADS):
        part = features_of(head)
        grad_scores.append(halves(jnp.where(mask, product(grads[head], v_ref[:, part], NT), 0.0)))
        dq = product(grad_scores[head], keys[head], NN) + product(grads[head], halves(prefix_ref[head]), NT)
        dq_ref[:, part] = slope(q_ref[:, part]) * dq
    write(dq_ref, dq_out)
    for head in range(HEADS):
        part = features_of(head)
        query = halves(feature(q_ref[:, part]))
        dk = product(grad_scores[head], query, TN) + product(v_ref[:, part], suffixes[head], NT)
        dk_ref[:, part] = slope(k_ref[:, part]) * dk
    write(dk_ref, dk_out)
    for head in range(HEADS):
        part = features_of(head)
        dv = product(halves(scores_ref[head]), grads[head], TN) + product(keys[head], suffixes[head], NN)
        dv_ref[:, part] = dv
    write(dv_ref, dv_out)
    for copy in copies:
        copy.wait()


def call(kernel, outs, *operands, scalars=0, inputs=VMEM, outputs=VMEM, scratch=()):
    return pl.pallas_call(
        kernel,
        out_shape=[jax.ShapeDtypeStruct(shape, dtype) for shape, dtype in outs],
        in_specs=[SMEM] * scalars + [inputs] * (len(operands) - scalars),
        out_specs=[outputs] * len(outs),
        scratch_shapes=scratch,
        compiler_params=pltpu.CompilerParams(vmem_limit_bytes=8 << 20),
    )(*operands)


def scan_devices(at, states, backward):
    blocks, x_size, members = lax.axis_size("zb"), lax.axis_size("x"), lax.axis_size(NEAR)
    core = lax.axis_index("c")
    piece = (HEADS * HD // members, HD)
    flat, near, far = (members,) + piece, (x_size, members // x_size) + piece, (x_size,) + piece
    cores = lax.all_gather(states, "c")

    def scatter(cores):
        pieces = lax.all_to_all((cores[0] + cores[1]).reshape(flat), NEAR, 0, 0).reshape(near)
        return tuple(call(total_kernel, [(near, F32), (far, F32)], pieces))

    def idle(cores):
        return jnp.zeros(near, F32), jnp.zeros(far, F32)

    pieces, total = lax.cond(core == 1, scatter, idle, cores)
    steps = sorted(range(1, blocks), key=lambda step: -min(step, blocks - step))
    totals = [
        lax.ppermute(total, ("zb", "c"), [(2 * block + 1, 2 * ((block + step) % blocks)) for block in range(blocks)])
        for step in steps
    ]
    pieces = lax.all_gather(pieces, "c")

    def gather(operands):
        kernel = functools.partial(prefix_kernel, backward, steps)
        (sums,) = call(kernel, [(near, F32)], at, *operands, scalars=1)
        return lax.all_to_all(sums.reshape(flat), NEAR, 0, 0).reshape(HEADS, HD, HD)

    sums = lax.cond(core == 0, gather, lambda operands: jnp.zeros((HEADS, HD, HD), F32), [pieces, *totals])
    return lax.all_gather(sums, "c"), cores


def body(query, key, value, gain, grad_out):
    tokens = query.shape[0]
    at = lax.axis_index(("x", "zb", "zp", "c")).reshape(1)
    wide, per_head, state = (tokens, HEADS * HD), (HEADS, tokens, HD), ((HEADS, HD, HD), F32)
    given = (key, value, query, grad_out, gain.reshape(HEADS, HD))
    k, v, q, g, gain, states = call(
        local_kernel,
        [(wide, BF16)] * 4 + [((HEADS, HD), F32), state],
        at,
        *(pltpu.with_memory_space_constraint(array, pltpu.HBM) for array in given),
        scalars=1,
        inputs=HBM,
        scratch=[pltpu.SemaphoreType.DMA((5,))],
    )
    earlier = scan_devices(at, states, False)
    scores, grad, prefix, states = call(
        forward_kernel,
        [((HEADS, tokens, tokens), F32), (per_head, F32), state, state],
        *(at, q, k, v, g, gain, *earlier),
        scalars=1,
    )
    later = scan_devices(at, states, True)
    return tuple(
        call(
            backward_kernel,
            [(wide, F32)] * 3,
            *(at, q, k, v, scores, grad, prefix, *later),
            scalars=1,
            outputs=HBM,
            scratch=[pltpu.VMEM(wide, F32)] * 3 + [pltpu.SemaphoreType.DMA((3,))],
        )
    )


def over(devices):
    mesh = Mesh(devices, ("x", "zb", "zp", "c", "h"))
    placed = P(("x", "zb", "zp", "c"), "h")
    return jax.shard_map(
        body,
        mesh=mesh,
        in_specs=(placed, placed, placed, P("h"), placed),
        out_specs=(placed, placed, placed),
        check_vma=False,
    )


def solution(mesh):
    seq, head = mesh.devices.shape
    return over(mesh.devices.reshape(4, 4, seq // 32, 2, head))
```

```python
import functools

import jax
import jax.numpy as jnp
from jax import lax
from jax.experimental import pallas as pl
from jax.experimental.pallas import tpu as pltpu
from jax.sharding import Mesh, PartitionSpec as P

HD = 128
HEADS = 2
F32 = jnp.float32
BF16 = jnp.bfloat16
VMEM = pl.BlockSpec(memory_space=pltpu.VMEM)
SMEM = pl.BlockSpec(memory_space=pltpu.SMEM)
HBM = pl.BlockSpec(memory_space=pltpu.HBM)
NN = (((1,), (0,)), ((), ()))
NT = (((1,), (1,)), ((), ()))
TN = (((0,), (0,)), ((), ()))
NEAR = ("x", "zp")


def halves(wide):
    high = wide.astype(BF16)
    low = (wide - high.astype(F32)).astype(BF16)
    return high, low


def one(left, right, dims):
    return lax.dot_general(left, right, dims, preferred_element_type=F32)


def product(left, right, dims):
    if not isinstance(left, tuple):
        return one(left, right[0], dims) + one(left, right[1], dims)
    if not isinstance(right, tuple):
        return one(left[0], right, dims) + one(left[1], right, dims)
    return one(left[0], right[0], dims) + (one(left[0], right[1], dims) + one(left[1], right[0], dims))


def feature(raw):
    wide = raw.astype(F32)
    return jnp.where(wide > 0, wide + 1.0, jnp.exp(jnp.minimum(wide, 0.0)))


def slope(raw):
    wide = raw.astype(F32)
    return jnp.where(wide > 0, 1.0, jnp.exp(jnp.minimum(wide, 0.0)))


def causal(size):
    row = lax.broadcasted_iota(jnp.int32, (size, size), 0)
    column = lax.broadcasted_iota(jnp.int32, (size, size), 1)
    return row >= column


def features_of(head):
    return slice(head * HD, head * HD + HD)


def local_kernel(at_ref, k_in, v_in, q_in, g_in, gain_in, k_ref, v_ref, q_ref, first_ref, g_ref, gain_ref, sems):
    pairs = ((k_in, k_ref), (v_in, v_ref), (g_in, g_ref), (gain_in, gain_ref), (q_in, q_ref))
    copies = [pltpu.make_async_copy(start, end, sems.at[place]) for place, (start, end) in enumerate(pairs)]
    for copy in copies:
        copy.start()
    copies[0].wait()
    copies[1].wait()
    for head in range(HEADS):
        part = features_of(head)
        first_ref[head] = product(halves(feature(k_ref[:, part])), v_ref[:, part], TN)
    for copy in copies[2:]:
        copy.wait()
    for head in range(HEADS):
        first_ref[HEADS + head] = gain_ref[head : head + 1, :] * g_ref[:, features_of(head)].astype(F32)


def core_of(at_ref):
    return lax.rem(at_ref[0], 2)


def total_kernel(pieces_ref, copy_ref, out_ref):
    copy_ref[...] = pieces_ref[...]
    total = pieces_ref[:, 0]
    for place in range(1, pieces_ref.shape[1]):
        total = total + pieces_ref[:, place]
    out_ref[...] = total


def total_and_pack_kernel(pieces_ref, prefix_ref, grad_ref, third_ref, out_ref):
    x_size, place_size, rows = pieces_ref.shape[:3]
    each = HD // rows
    for x in range(x_size):
        total = pieces_ref[x, 0]
        for place in range(1, place_size):
            total = total + pieces_ref[x, place]
        out_ref[x] = total
        for place in range(place_size):
            member = x * place_size + place
            third_ref[member // each, pl.ds(member % each * rows, rows), :] = pieces_ref[x, place]
    third_ref[HEADS : 2 * HEADS] = prefix_ref[...]
    third_ref[2 * HEADS :] = grad_ref[...]


def prefix_kernel(backward, steps, place_size, source, at_ref, pieces_ref, *refs):
    far_refs, out_ref = refs[:-1], refs[-1]
    x_size, rows = far_refs[0].shape[:2]
    each = HD // rows
    blocks = len(steps) + 1
    block = lax.rem(lax.div(at_ref[0], 2 * place_size), blocks)
    base = jnp.zeros((rows, HD), F32)
    for x in range(x_size)[:: -1 if backward else 1]:
        so_far = row = base
        for step, far_ref in zip(steps, far_refs):
            other = lax.rem(block + blocks - step, blocks)
            total = far_ref[x]
            row = row + total
            so_far = so_far + jnp.where(other > block if backward else other < block, total, 0.0)
        for place in range(place_size)[:: -1 if backward else 1]:
            member = x * place_size + place
            piece = pieces_ref[source, member // each, pl.ds(member % each * rows, rows), :]
            out_ref[x, place] = so_far
            so_far = so_far + piece
            row = row + piece
        base = row


def scores_kernel(q_ref, k_ref, v_ref, pieces_ref, scores_ref, second_ref):
    mask = causal(q_ref.shape[0])
    second_ref[:HEADS] = pieces_ref[...]
    for head in range(HEADS):
        part = features_of(head)
        query = halves(feature(q_ref[:, part]))
        key = halves(feature(k_ref[:, part]))
        scores = jnp.where(mask, product(query, key, NT), 0.0)
        scores_ref[head] = scores
        second_ref[HEADS + head] = product(halves(scores), v_ref[:, part], NN)
        second_ref[2 * HEADS + head] = q_ref[:, part].astype(F32)


def forward_kernel(first_ref, second_ref, prefix_ref, grad0_ref, grad1_ref, chip_ref, other_ref):
    for head in range(HEADS):
        states = []
        for core in range(2):
            query = halves(feature(second_ref[core, 2 * HEADS + head]))
            prefix = prefix_ref[head]
            if core:
                prefix = prefix + first_ref[0, head]
            output = second_ref[core, HEADS + head] + product(query, halves(prefix), NN)
            inverse = lax.rsqrt(jnp.mean(output * output, axis=-1, keepdims=True) + 1e-06)
            normed = output * inverse
            scaled = first_ref[core, HEADS + head]
            grad = inverse * (scaled - normed * jnp.mean(scaled * normed, axis=-1, keepdims=True))
            (grad0_ref, grad1_ref)[core][head] = grad
            states.append(product(query, halves(grad), TN))
        chip_ref[head] = states[0] + states[1]
        other_ref[head] = states[1]


def backward_kernel(at_ref, *refs):
    q_ref, k_ref, v_ref, scores_ref, grad_ref, other_ref, first_ref, third_ref, last_ref = refs[:9]
    dq_out, dk_out, dv_out, dq_ref, dk_ref, dv_ref, sems = refs[9:]
    mask = causal(q_ref.shape[0])
    late = core_of(at_ref) == 1
    copies = []

    def write(start, end):
        copies.append(pltpu.make_async_copy(start, end, sems.at[len(copies)]))
        copies[-1].start()

    heads = range(HEADS)
    grads = [halves(jnp.where(late, third_ref[0, 2 * HEADS + head], grad_ref[head])) for head in heads]
    prefixes = [halves(third_ref[0, HEADS + head] + jnp.where(late, first_ref[0, head], 0.0)) for head in heads]
    suffixes = [halves(last_ref[1, head] + jnp.where(late, 0.0, other_ref[head])) for head in heads]
    keys = [halves(feature(k_ref[:, features_of(head)])) for head in heads]
    grad_scores = []
    for head in heads:
        part = features_of(head)
        grad_scores.append(halves(jnp.where(mask, product(grads[head], v_ref[:, part], NT), 0.0)))
        dq = product(grad_scores[head], keys[head], NN) + product(grads[head], prefixes[head], NT)
        dq_ref[:, part] = slope(q_ref[:, part]) * dq
    write(dq_ref, dq_out)
    for head in heads:
        part = features_of(head)
        query = halves(feature(q_ref[:, part]))
        dk = product(grad_scores[head], query, TN) + product(v_ref[:, part], suffixes[head], NT)
        dk_ref[:, part] = slope(k_ref[:, part]) * dk
    write(dk_ref, dk_out)
    for head in heads:
        part = features_of(head)
        dv = product(halves(scores_ref[head]), grads[head], TN) + product(keys[head], suffixes[head], NN)
        dv_ref[:, part] = dv
    write(dv_ref, dv_out)
    for copy in copies:
        copy.wait()


def call(kernel, outs, *operands, scalars=0, inputs=VMEM, outputs=VMEM, scratch=()):
    return pl.pallas_call(
        kernel,
        out_shape=[jax.ShapeDtypeStruct(shape, dtype) for shape, dtype in outs],
        in_specs=[SMEM] * scalars + [inputs] * (len(operands) - scalars),
        out_specs=[outputs] * len(outs),
        scratch_shapes=scratch,
        compiler_params=pltpu.CompilerParams(vmem_limit_bytes=8 << 20),
    )(*operands)


def body(query, key, value, gain, grad_out):
    tokens = query.shape[0]
    at = lax.axis_index(("x", "zb", "zp", "c")).reshape(1)
    core = lax.axis_index("c")
    blocks, x_size, place_size = lax.axis_size("zb"), lax.axis_size("x"), lax.axis_size("zp")
    members = x_size * place_size
    piece = (HEADS * HD // members, HD)
    flat, near, far = (members,) + piece, (x_size, place_size) + piece, (x_size,) + piece
    state, three, wide = (HEADS, HD, HD), (3 * HEADS, HD, HD), (tokens, HEADS * HD)
    steps = sorted(range(1, blocks), key=lambda step: min(step, blocks - step))

    def within(pieces, shape):
        return lax.all_to_all(pieces.reshape(flat), NEAR, 0, 0).reshape(shape)

    def to_blocks(total, source):
        ends = [(step, [(2 * block + source, 2 * ((block + step) % blocks) + 1 - source) for block in range(blocks)]) for step in steps]
        return [lax.ppermute(total, ("zb", "c"), pairs) for step, pairs in ends]

    def none(*shapes):
        return lambda *operands: tuple(jnp.zeros(shape, F32) for shape in shapes)

    def sums(backward, source, pieces, totals):
        kernel = functools.partial(prefix_kernel, backward, steps, place_size, source)
        return within(call(kernel, [(near, F32)], at, pieces, *totals, scalars=1)[0], state)

    given = (key, value, query, grad_out, gain.reshape(HEADS, HD))
    k, v, q, first = call(
        local_kernel,
        [(wide, BF16)] * 3 + [((2 * HEADS, HD, HD), F32)],
        at,
        *(pltpu.with_memory_space_constraint(array, pltpu.HBM) for array in given),
        scalars=1,
        inputs=HBM,
        scratch=[pltpu.VMEM(wide, BF16), pltpu.VMEM((HEADS, HD), F32), pltpu.SemaphoreType.DMA((5,))],
    )
    firsts = lax.all_gather(first, "c")

    def start(firsts):
        chip = firsts[0, :HEADS] + firsts[1, :HEADS]
        return tuple(call(total_kernel, [(near, F32), (far, F32)], within(chip, near)))

    pieces, total = lax.cond(core == 1, start, none(near, far), firsts)
    totals = to_blocks(total, 1)
    scores, second = call(scores_kernel, [(state, F32), (three, F32)], q, k, v, pieces.reshape(state))
    seconds = lax.all_gather(second, "c")

    def middle(firsts, seconds, totals):
        prefix = sums(False, 1, seconds, totals)
        grad0, grad1, chip, other = call(forward_kernel, [(state, F32)] * 4, firsts, seconds, prefix)
        third, total = call(total_and_pack_kernel, [(three, F32), (far, F32)], within(chip, near), prefix, grad1)
        return third, total, grad0, other

    third, total, grad, other = lax.cond(core == 0, middle, none(three, far, state, state), firsts, seconds, totals)
    totals = to_blocks(total, 0)
    thirds = lax.all_gather(third, "c")

    def end(thirds, totals):
        return (sums(True, 0, thirds, totals),)

    (last,) = lax.cond(core == 1, end, none(state), thirds, totals)
    lasts = lax.all_gather(last, "c")
    return tuple(
        call(
            backward_kernel,
            [(wide, F32)] * 3,
            *(at, q, k, v, scores, grad, other, firsts, thirds, lasts),
            scalars=1,
            outputs=HBM,
            scratch=[pltpu.VMEM(wide, F32)] * 3 + [pltpu.SemaphoreType.DMA((3,))],
        )
    )


def over(devices):
    mesh = Mesh(devices, ("x", "zb", "zp", "c", "h"))
    placed = P(("x", "zb", "zp", "c"), "h")
    return jax.shard_map(
        body,
        mesh=mesh,
        in_specs=(placed, placed, placed, P("h"), placed),
        out_specs=(placed, placed, placed),
        check_vma=False,
    )


def solution(mesh):
    seq, head = mesh.devices.shape
    return over(mesh.devices.reshape(4, 4, seq // 32, 2, head))
```

```python
import functools

import jax
import jax.numpy as jnp
from jax import lax
from jax.experimental import pallas as pl
from jax.experimental.pallas import tpu as pltpu
from jax.sharding import Mesh, PartitionSpec as P

HD = 128
HEADS = 2
F32 = jnp.float32
BF16 = jnp.bfloat16
VMEM = pl.BlockSpec(memory_space=pltpu.VMEM)
SMEM = pl.BlockSpec(memory_space=pltpu.SMEM)
HBM = pl.BlockSpec(memory_space=pltpu.HBM)
NN = (((1,), (0,)), ((), ()))
NT = (((1,), (1,)), ((), ()))
TN = (((0,), (0,)), ((), ()))
SEQ = ("x", "zb", "zp", "c")


def halves(wide):
    high = wide.astype(BF16)
    low = (wide - high.astype(F32)).astype(BF16)
    return high, low


def one(left, right, dims):
    return lax.dot_general(left, right, dims, preferred_element_type=F32)


def product(left, right, dims):
    if not isinstance(left, tuple):
        return one(left, right[0], dims) + one(left, right[1], dims)
    if not isinstance(right, tuple):
        return one(left[0], right, dims) + one(left[1], right, dims)
    return one(left[0], right[0], dims) + (one(left[0], right[1], dims) + one(left[1], right[0], dims))


def feature(raw):
    wide = raw.astype(F32)
    return jnp.where(wide > 0, wide + 1.0, jnp.exp(jnp.minimum(wide, 0.0)))


def slope(raw):
    wide = raw.astype(F32)
    return jnp.where(wide > 0, 1.0, jnp.exp(jnp.minimum(wide, 0.0)))


def causal(size):
    row = lax.broadcasted_iota(jnp.int32, (size, size), 0)
    column = lax.broadcasted_iota(jnp.int32, (size, size), 1)
    return row >= column


def features_of(head):
    return slice(head * HD, head * HD + HD)


def local_kernel(at_ref, k_in, v_in, q_in, g_in, gain_in, k_ref, v_ref, q_ref, first_ref, g_ref, gain_ref, sems):
    pairs = ((k_in, k_ref), (v_in, v_ref), (g_in, g_ref), (gain_in, gain_ref), (q_in, q_ref))
    copies = [pltpu.make_async_copy(start, end, sems.at[place]) for place, (start, end) in enumerate(pairs)]
    for copy in copies:
        copy.start()
    copies[0].wait()
    copies[1].wait()
    for head in range(HEADS):
        part = features_of(head)
        first_ref[head] = product(halves(feature(k_ref[:, part])), v_ref[:, part], TN)
    for copy in copies[2:]:
        copy.wait()
    for head in range(HEADS):
        first_ref[HEADS + head] = gain_ref[head : head + 1, :] * g_ref[:, features_of(head)].astype(F32)


def core_of(at_ref):
    return lax.rem(at_ref[0], 2)


def total_kernel(pieces_ref, copy_ref, out_ref):
    copy_ref[...] = pieces_ref[...]
    total = pieces_ref[:, 0]
    for place in range(1, pieces_ref.shape[1]):
        total = total + pieces_ref[:, place]
    out_ref[...] = total


def total_and_pack_kernel(pieces_ref, prefix_ref, grad_ref, third_ref, out_ref):
    x_size, place_size, rows = pieces_ref.shape[:3]
    each = HD // rows
    for x in range(x_size):
        total = pieces_ref[x, 0]
        for place in range(1, place_size):
            total = total + pieces_ref[x, place]
        out_ref[x] = total
        for place in range(place_size):
            member = x * place_size + place
            third_ref[member // each, pl.ds(member % each * rows, rows), :] = pieces_ref[x, place]
    third_ref[HEADS : 2 * HEADS] = prefix_ref[...]
    third_ref[2 * HEADS :] = grad_ref[...]


def slots(place_size):
    return (1, 0) + tuple(range(2, place_size))


def prefix_kernel(backward, steps, place_size, source, at_ref, pieces_ref, *refs):
    far_refs, out_ref = refs[:-1], refs[-1]
    x_size, rows = far_refs[0].shape[:2]
    each = HD // rows
    blocks = len(steps) + 1
    block = lax.rem(lax.div(at_ref[0], 2 * place_size), blocks)
    base = jnp.zeros((rows, HD), F32)
    for x in range(x_size)[:: -1 if backward else 1]:
        so_far = row = base
        for step, far_ref in zip(steps, far_refs):
            other = lax.rem(block + blocks - step, blocks)
            total = far_ref[x]
            row = row + total
            so_far = so_far + jnp.where(other > block if backward else other < block, total, 0.0)
        for place in range(place_size)[:: -1 if backward else 1]:
            slot = slots(place_size)[place]
            member = x * place_size + slot
            piece = pieces_ref[source, member // each, pl.ds(member % each * rows, rows), :]
            out_ref[x, slot] = so_far
            so_far = so_far + piece
            row = row + piece
        base = row


def scores_kernel(q_ref, k_ref, v_ref, pieces_ref, scores_ref, second_ref):
    mask = causal(q_ref.shape[0])
    second_ref[:HEADS] = pieces_ref[...]
    for head in range(HEADS):
        part = features_of(head)
        query = halves(feature(q_ref[:, part]))
        key = halves(feature(k_ref[:, part]))
        scores = jnp.where(mask, product(query, key, NT), 0.0)
        scores_ref[head] = scores
        second_ref[HEADS + head] = product(halves(scores), v_ref[:, part], NN)
        second_ref[2 * HEADS + head] = q_ref[:, part].astype(F32)


def forward_kernel(first_ref, second_ref, prefix_ref, grad0_ref, grad1_ref, chip_ref, other_ref):
    for head in range(HEADS):
        states = []
        for core in range(2):
            query = halves(feature(second_ref[core, 2 * HEADS + head]))
            prefix = prefix_ref[head]
            if core:
                prefix = prefix + first_ref[0, head]
            output = second_ref[core, HEADS + head] + product(query, halves(prefix), NN)
            inverse = lax.rsqrt(jnp.mean(output * output, axis=-1, keepdims=True) + 1e-06)
            normed = output * inverse
            scaled = first_ref[core, HEADS + head]
            grad = inverse * (scaled - normed * jnp.mean(scaled * normed, axis=-1, keepdims=True))
            (grad0_ref, grad1_ref)[core][head] = grad
            states.append(product(query, halves(grad), TN))
        chip_ref[head] = states[0] + states[1]
        other_ref[head] = states[1]


def inner_kernel(at_ref, *refs):
    q_ref, k_ref, v_ref, scores_ref, grad_ref, first_ref, third_ref, dq_ref, dk_ref, dv_ref = refs
    mask = causal(q_ref.shape[0])
    late = core_of(at_ref) == 1
    for head in range(HEADS):
        part = features_of(head)
        query = halves(feature(q_ref[:, part]))
        key = halves(feature(k_ref[:, part]))
        grad = halves(jnp.where(late, third_ref[0, 2 * HEADS + head], grad_ref[head]))
        prefix = halves(third_ref[0, HEADS + head] + jnp.where(late, first_ref[0, head], 0.0))
        grad_scores = halves(jnp.where(mask, product(grad, v_ref[:, part], NT), 0.0))
        dq_ref[:, part] = slope(q_ref[:, part]) * (product(grad_scores, key, NN) + product(grad, prefix, NT))
        dk_ref[:, part] = product(grad_scores, query, TN)
        dv_ref[:, part] = product(halves(scores_ref[head]), grad, TN)


def backward_kernel(at_ref, k_ref, v_ref, near_dk_ref, near_dv_ref, other_ref, last_ref, dk_out, dv_out, dk_ref, dv_ref, sems):
    late = core_of(at_ref) == 1
    suffixes = [halves(last_ref[1, head] + jnp.where(late, 0.0, other_ref[head])) for head in range(HEADS)]
    copies = [pltpu.make_async_copy(dk_ref, dk_out, sems.at[0]), pltpu.make_async_copy(dv_ref, dv_out, sems.at[1])]
    for head in range(HEADS):
        part = features_of(head)
        raw = k_ref[:, part]
        dk_ref[:, part] = slope(raw) * (near_dk_ref[:, part] + product(v_ref[:, part], suffixes[head], NT))
    copies[0].start()
    for head in range(HEADS):
        part = features_of(head)
        dv_ref[:, part] = near_dv_ref[:, part] + product(halves(feature(k_ref[:, part])), suffixes[head], NN)
    copies[1].start()
    for copy in copies:
        copy.wait()


def call(kernel, outs, *operands, scalars=0, inputs=VMEM, outputs=VMEM, scratch=()):
    return pl.pallas_call(
        kernel,
        out_shape=[jax.ShapeDtypeStruct(shape, dtype) for shape, dtype in outs],
        in_specs=[SMEM] * scalars + [inputs] * (len(operands) - scalars),
        out_specs=[outputs] * len(outs),
        scratch_shapes=scratch,
        compiler_params=pltpu.CompilerParams(vmem_limit_bytes=8 << 20),
    )(*operands)


def body(query, key, value, gain, grad_out):
    tokens = query.shape[0]
    at = lax.axis_index(SEQ).reshape(1)
    core = lax.axis_index("c")
    blocks, x_size, place_size = lax.axis_size("zb"), lax.axis_size("x"), lax.axis_size("zp")
    members = x_size * place_size
    piece = (HEADS * HD // members, HD)
    flat, near, far = (members,) + piece, (x_size, place_size) + piece, (x_size,) + piece
    state, three, wide = (HEADS, HD, HD), (3 * HEADS, HD, HD), (tokens, HEADS * HD)
    steps = sorted(range(1, blocks), key=lambda step: min(step, blocks - step))

    leading = sorted(range(place_size), key=lambda place: slots(place_size)[place])
    groups = [
        [((x * blocks + block) * place_size + place) * 2 + one_core for x in range(x_size) for place in leading]
        for block in range(blocks)
        for one_core in range(2)
    ]

    def within(pieces, shape):
        return lax.all_to_all(pieces.reshape(flat), SEQ, 0, 0, axis_index_groups=groups).reshape(shape)

    def to_blocks(total, source):
        ends = [(step, [(2 * block + source, 2 * ((block + step) % blocks) + 1 - source) for block in range(blocks)]) for step in steps]
        return [lax.ppermute(total, ("zb", "c"), pairs) for step, pairs in ends]

    def none(*shapes):
        return lambda *operands: tuple(jnp.zeros(shape, F32) for shape in shapes)

    def sums(backward, source, pieces, totals):
        kernel = functools.partial(prefix_kernel, backward, steps, place_size, source)
        return within(call(kernel, [(near, F32)], at, pieces, *totals, scalars=1)[0], state)

    given = (key, value, query, grad_out, gain.reshape(HEADS, HD))
    k, v, q, first = call(
        local_kernel,
        [(wide, BF16)] * 3 + [((2 * HEADS, HD, HD), F32)],
        at,
        *(pltpu.with_memory_space_constraint(array, pltpu.HBM) for array in given),
        scalars=1,
        inputs=HBM,
        scratch=[pltpu.VMEM(wide, BF16), pltpu.VMEM((HEADS, HD), F32), pltpu.SemaphoreType.DMA((5,))],
    )
    firsts = lax.all_gather(first, "c")

    def start(firsts):
        chip = firsts[0, :HEADS] + firsts[1, :HEADS]
        return tuple(call(total_kernel, [(near, F32), (far, F32)], within(chip, near)))

    pieces, total = lax.cond(core == 1, start, none(near, far), firsts)
    totals = to_blocks(total, 1)
    scores, second = call(scores_kernel, [(state, F32), (three, F32)], q, k, v, pieces.reshape(state))
    seconds = lax.all_gather(second, "c")

    def middle(firsts, seconds, totals):
        prefix = sums(False, 1, seconds, totals)
        grad0, grad1, chip, other = call(forward_kernel, [(state, F32)] * 4, firsts, seconds, prefix)
        third, total = call(total_and_pack_kernel, [(three, F32), (far, F32)], within(chip, near), prefix, grad1)
        return third, total, grad0, other

    third, total, grad, other = lax.cond(core == 0, middle, none(three, far, state, state), firsts, seconds, totals)
    totals = to_blocks(total, 0)
    thirds = lax.all_gather(third, "c")
    dq, dk, dv = call(inner_kernel, [(wide, F32)] * 3, at, q, k, v, scores, grad, firsts, thirds, scalars=1)

    def end(thirds, totals):
        return (sums(True, 0, thirds, totals),)

    (last,) = lax.cond(core == 1, end, none(state), thirds, totals)
    lasts = lax.all_gather(last, "c")
    dk, dv = call(
        backward_kernel,
        [(wide, F32)] * 2,
        *(at, k, v, dk, dv, other, lasts),
        scalars=1,
        outputs=HBM,
        scratch=[pltpu.VMEM(wide, F32)] * 2 + [pltpu.SemaphoreType.DMA((2,))],
    )
    return dq, dk, dv


def over(devices):
    mesh = Mesh(devices, ("x", "zb", "zp", "c", "h"))
    placed = P(("x", "zb", "zp", "c"), "h")
    return jax.shard_map(
        body,
        mesh=mesh,
        in_specs=(placed, placed, placed, P("h"), placed),
        out_specs=(placed, placed, placed),
        check_vma=False,
    )


def solution(mesh):
    seq, head = mesh.devices.shape
    return over(mesh.devices.reshape(4, 4, seq // 32, 2, head))
```

```python
import functools

import jax
import jax.numpy as jnp
from jax import lax
from jax.experimental import pallas as pl
from jax.experimental.pallas import tpu as pltpu
from jax.sharding import Mesh, PartitionSpec as P

HD = 128
HEADS = 2
F32 = jnp.float32
BF16 = jnp.bfloat16
VMEM = pl.BlockSpec(memory_space=pltpu.VMEM)
SMEM = pl.BlockSpec(memory_space=pltpu.SMEM)
HBM = pl.BlockSpec(memory_space=pltpu.HBM)
NN = (((1,), (0,)), ((), ()))
NT = (((1,), (1,)), ((), ()))
TN = (((0,), (0,)), ((), ()))
SEQ = ("x", "zb", "zp", "c")


def halves(wide):
    high = wide.astype(BF16)
    low = (wide - high.astype(F32)).astype(BF16)
    return high, low


def one(left, right, dims):
    return lax.dot_general(left, right, dims, preferred_element_type=F32)


def product(left, right, dims):
    if not isinstance(left, tuple):
        return one(left, right[0], dims) + one(left, right[1], dims)
    if not isinstance(right, tuple):
        return one(left[0], right, dims) + one(left[1], right, dims)
    return one(left[0], right[0], dims) + (one(left[0], right[1], dims) + one(left[1], right[0], dims))


def feature(raw):
    wide = raw.astype(F32)
    return jnp.where(wide > 0, wide + 1.0, jnp.exp(jnp.minimum(wide, 0.0)))


def slope(raw):
    wide = raw.astype(F32)
    return jnp.where(wide > 0, 1.0, jnp.exp(jnp.minimum(wide, 0.0)))


def causal(size):
    row = lax.broadcasted_iota(jnp.int32, (size, size), 0)
    column = lax.broadcasted_iota(jnp.int32, (size, size), 1)
    return row >= column


def features_of(head):
    return slice(head * HD, head * HD + HD)


def local_kernel(at_ref, k_in, v_in, q_in, g_in, gain_in, k_ref, v_ref, q_ref, first_ref, g_ref, gain_ref, sems):
    pairs = ((k_in, k_ref), (v_in, v_ref), (g_in, g_ref), (gain_in, gain_ref), (q_in, q_ref))
    copies = [pltpu.make_async_copy(start, end, sems.at[place]) for place, (start, end) in enumerate(pairs)]
    for copy in copies:
        copy.start()
    copies[0].wait()
    copies[1].wait()
    for head in range(HEADS):
        part = features_of(head)
        first_ref[head] = product(halves(feature(k_ref[:, part])), v_ref[:, part], TN)
    for copy in copies[2:]:
        copy.wait()
    for head in range(HEADS):
        first_ref[HEADS + head] = gain_ref[head : head + 1, :] * g_ref[:, features_of(head)].astype(F32)


def core_of(at_ref):
    return lax.rem(at_ref[0], 2)


def total_kernel(pieces_ref, copy_ref, out_ref):
    copy_ref[...] = pieces_ref[...]
    total = pieces_ref[:, 0]
    for place in range(1, pieces_ref.shape[1]):
        total = total + pieces_ref[:, place]
    out_ref[...] = total


def total_and_pack_kernel(pieces_ref, prefix_ref, grad_ref, third_ref, out_ref):
    x_size, place_size, rows = pieces_ref.shape[:3]
    each = HD // rows
    for x in range(x_size):
        total = pieces_ref[x, 0]
        for place in range(1, place_size):
            total = total + pieces_ref[x, place]
        out_ref[x] = total
        for place in range(place_size):
            member = x * place_size + place
            third_ref[member // each, pl.ds(member % each * rows, rows), :] = pieces_ref[x, place]
    third_ref[HEADS : 2 * HEADS] = prefix_ref[...]
    third_ref[2 * HEADS :] = grad_ref[...]


def slots(place_size):
    return (1, 0) + tuple(range(2, place_size))


def prefix_kernel(backward, steps, place_size, source, at_ref, pieces_ref, *refs):
    far_refs, out_ref = refs[:-1], refs[-1]
    x_size, rows = far_refs[0].shape[:2]
    each = HD // rows
    blocks = len(steps) + 1
    block = lax.rem(lax.div(at_ref[0], 2 * place_size), blocks)
    base = jnp.zeros((rows, HD), F32)
    for x in range(x_size)[:: -1 if backward else 1]:
        so_far = row = base
        for step, far_ref in zip(steps, far_refs):
            other = lax.rem(block + blocks - step, blocks)
            total = far_ref[x]
            row = row + total
            so_far = so_far + jnp.where(other > block if backward else other < block, total, 0.0)
        for place in range(place_size)[:: -1 if backward else 1]:
            slot = slots(place_size)[place]
            member = x * place_size + slot
            piece = pieces_ref[source, member // each, pl.ds(member % each * rows, rows), :]
            out_ref[x, slot] = so_far
            so_far = so_far + piece
            row = row + piece
        base = row


def scores_kernel(at_ref, q_ref, k_ref, v_ref, pieces_ref, first_ref, scores_ref, second_ref):
    mask = causal(q_ref.shape[0])
    late = core_of(at_ref) == 1
    second_ref[:HEADS] = pieces_ref[...]
    for head in range(HEADS):
        part = features_of(head)
        wide = feature(q_ref[:, part])
        query = halves(wide)
        key = halves(feature(k_ref[:, part]))
        scores = jnp.where(mask, product(query, key, NT), 0.0)
        scores_ref[head] = scores
        before = halves(jnp.where(late, first_ref[0, head], 0.0))
        second_ref[HEADS + head] = product(halves(scores), v_ref[:, part], NN) + product(query, before, NN)
        second_ref[2 * HEADS + head] = wide


def split_kernel(second_ref, high_ref, low_ref, high_t_ref, low_t_ref):
    for head in range(HEADS):
        wide = second_ref[:, 2 * HEADS + head].reshape(2 * HD, HD)
        high_ref[head], low_ref[head] = halves(wide)
        high_t_ref[head], low_t_ref[head] = halves(wide.T)


def forward_kernel(first_ref, second_ref, high_ref, low_ref, high_t_ref, low_t_ref, prefix_ref, grad0_ref, grad1_ref, chip_ref):
    for head in range(HEADS):
        rows = (2 * HD, HD)
        query = high_ref[head], low_ref[head]
        output = second_ref[:, HEADS + head].reshape(rows) + product(query, halves(prefix_ref[head]), NN)
        inverse = lax.rsqrt(jnp.mean(output * output, axis=-1, keepdims=True) + 1e-06)
        normed = output * inverse
        scaled = first_ref[:, HEADS + head].reshape(rows)
        grad = inverse * (scaled - normed * jnp.mean(scaled * normed, axis=-1, keepdims=True))
        chip_ref[head] = product((high_t_ref[head], low_t_ref[head]), halves(grad), NN)
        grad0_ref[head] = grad[:HD]
        grad1_ref[head] = grad[HD:]


def inner_kernel(at_ref, *refs):
    q_ref, k_ref, v_ref, scores_ref, grad_ref, first_ref, second_ref, third_ref, dq_ref, dk_ref, dv_ref, other_ref = refs
    mask = causal(q_ref.shape[0])
    late = core_of(at_ref) == 1
    for head in range(HEADS):
        part = features_of(head)
        query = halves(feature(q_ref[:, part]))
        key = halves(feature(k_ref[:, part]))
        grad = halves(jnp.where(late, third_ref[0, 2 * HEADS + head], grad_ref[head]))
        prefix = halves(third_ref[0, HEADS + head] + jnp.where(late, first_ref[0, head], 0.0))
        grad_scores = halves(jnp.where(mask, product(grad, v_ref[:, part], NT), 0.0))
        dq_ref[:, part] = slope(q_ref[:, part]) * (product(grad_scores, key, NN) + product(grad, prefix, NT))
        dk_ref[:, part] = product(grad_scores, query, TN)
        dv_ref[:, part] = product(halves(scores_ref[head]), grad, TN)
        later = halves(second_ref[1, 2 * HEADS + head]), halves(third_ref[0, 2 * HEADS + head])
        other_ref[head] = product(*later, TN)


def backward_kernel(at_ref, k_ref, v_ref, near_dk_ref, near_dv_ref, other_ref, last_ref, dk_out, dv_out, dk_ref, dv_ref, sems):
    late = core_of(at_ref) == 1
    suffixes = [halves(last_ref[1, head] + jnp.where(late, 0.0, other_ref[head])) for head in range(HEADS)]
    copies = [pltpu.make_async_copy(dk_ref, dk_out, sems.at[0]), pltpu.make_async_copy(dv_ref, dv_out, sems.at[1])]
    for head in range(HEADS):
        part = features_of(head)
        raw = k_ref[:, part]
        dk_ref[:, part] = slope(raw) * (near_dk_ref[:, part] + product(v_ref[:, part], suffixes[head], NT))
    copies[0].start()
    for head in range(HEADS):
        part = features_of(head)
        dv_ref[:, part] = near_dv_ref[:, part] + product(halves(feature(k_ref[:, part])), suffixes[head], NN)
    copies[1].start()
    for copy in copies:
        copy.wait()


def call(kernel, outs, *operands, scalars=0, inputs=VMEM, outputs=VMEM, scratch=()):
    return pl.pallas_call(
        kernel,
        out_shape=[jax.ShapeDtypeStruct(shape, dtype) for shape, dtype in outs],
        in_specs=[SMEM] * scalars + [inputs] * (len(operands) - scalars),
        out_specs=[outputs] * len(outs),
        scratch_shapes=scratch,
        compiler_params=pltpu.CompilerParams(vmem_limit_bytes=8 << 20),
    )(*operands)


def body(query, key, value, gain, grad_out):
    tokens = query.shape[0]
    at = lax.axis_index(SEQ).reshape(1)
    core = lax.axis_index("c")
    blocks, x_size, place_size = lax.axis_size("zb"), lax.axis_size("x"), lax.axis_size("zp")
    members = x_size * place_size
    piece = (HEADS * HD // members, HD)
    flat, near, far = (members,) + piece, (x_size, place_size) + piece, (x_size,) + piece
    state, three, wide = (HEADS, HD, HD), (3 * HEADS, HD, HD), (tokens, HEADS * HD)
    steps = sorted(range(1, blocks), key=lambda step: min(step, blocks - step))

    leading = sorted(range(place_size), key=lambda place: slots(place_size)[place])
    groups = [
        [((x * blocks + block) * place_size + place) * 2 + one_core for x in range(x_size) for place in leading]
        for block in range(blocks)
        for one_core in range(2)
    ]

    def within(pieces, shape):
        return lax.all_to_all(pieces.reshape(flat), SEQ, 0, 0, axis_index_groups=groups).reshape(shape)

    def to_blocks(total, source):
        ends = [(step, [(2 * block + source, 2 * ((block + step) % blocks) + 1 - source) for block in range(blocks)]) for step in steps]
        return [lax.ppermute(total, ("zb", "c"), pairs) for step, pairs in ends]

    def none(*shapes):
        return lambda *operands: tuple(jnp.zeros(shape, F32) for shape in shapes)

    def sums(backward, source, pieces, totals):
        kernel = functools.partial(prefix_kernel, backward, steps, place_size, source)
        return within(call(kernel, [(near, F32)], at, pieces, *totals, scalars=1)[0], state)

    given = (key, value, query, grad_out, gain.reshape(HEADS, HD))
    k, v, q, first = call(
        local_kernel,
        [(wide, BF16)] * 3 + [((2 * HEADS, HD, HD), F32)],
        at,
        *(pltpu.with_memory_space_constraint(array, pltpu.HBM) for array in given),
        scalars=1,
        inputs=HBM,
        scratch=[pltpu.VMEM(wide, BF16), pltpu.VMEM((HEADS, HD), F32), pltpu.SemaphoreType.DMA((5,))],
    )
    firsts = lax.all_gather(first, "c")

    def start(firsts):
        chip = firsts[0, :HEADS] + firsts[1, :HEADS]
        return tuple(call(total_kernel, [(near, F32), (far, F32)], within(chip, near)))

    pieces, total = lax.cond(core == 1, start, none(near, far), firsts)
    totals = to_blocks(total, 1)
    scores, second = call(scores_kernel, [(state, F32), (three, F32)], at, q, k, v, pieces.reshape(state), firsts, scalars=1)
    seconds = lax.all_gather(second, "c")
    tall, flat_t = ((HEADS, 2 * tokens, HD), BF16), ((HEADS, HD, 2 * tokens), BF16)
    queries = call(split_kernel, [tall, tall, flat_t, flat_t], seconds)

    def middle(firsts, seconds, queries, totals):
        prefix = sums(False, 1, seconds, totals)
        grad0, grad1, chip = call(forward_kernel, [(state, F32)] * 3, firsts, seconds, *queries, prefix)
        third, total = call(total_and_pack_kernel, [(three, F32), (far, F32)], within(chip, near), prefix, grad1)
        return third, total, grad0

    third, total, grad = lax.cond(core == 0, middle, none(three, far, state), firsts, seconds, queries, totals)
    totals = to_blocks(total, 0)
    thirds = lax.all_gather(third, "c")
    outs = [(wide, F32)] * 3 + [(state, F32)]
    dq, dk, dv, other = call(inner_kernel, outs, at, q, k, v, scores, grad, firsts, seconds, thirds, scalars=1)

    def end(thirds, totals):
        return (sums(True, 0, thirds, totals),)

    (last,) = lax.cond(core == 1, end, none(state), thirds, totals)
    lasts = lax.all_gather(last, "c")
    dk, dv = call(
        backward_kernel,
        [(wide, F32)] * 2,
        *(at, k, v, dk, dv, other, lasts),
        scalars=1,
        outputs=HBM,
        scratch=[pltpu.VMEM(wide, F32)] * 2 + [pltpu.SemaphoreType.DMA((2,))],
    )
    return dq, dk, dv


def over(devices):
    mesh = Mesh(devices, ("x", "zb", "zp", "c", "h"))
    placed = P(("x", "zb", "zp", "c"), "h")
    return jax.shard_map(
        body,
        mesh=mesh,
        in_specs=(placed, placed, placed, P("h"), placed),
        out_specs=(placed, placed, placed),
        check_vma=False,
    )


def solution(mesh):
    seq, head = mesh.devices.shape
    return over(mesh.devices.reshape(4, 4, seq // 32, 2, head))
```

```python
import functools

import jax
import jax.numpy as jnp
from jax import lax
from jax.experimental import pallas as pl
from jax.experimental.pallas import tpu as pltpu
from jax.sharding import Mesh, PartitionSpec as P

HD = 128
HEADS = 2
F32 = jnp.float32
BF16 = jnp.bfloat16
VMEM = pl.BlockSpec(memory_space=pltpu.VMEM)
SMEM = pl.BlockSpec(memory_space=pltpu.SMEM)
HBM = pl.BlockSpec(memory_space=pltpu.HBM)
NN = (((1,), (0,)), ((), ()))
NT = (((1,), (1,)), ((), ()))
TN = (((0,), (0,)), ((), ()))
SEQ = ("x", "zb", "zp", "c")


def halves(wide):
    high = wide.astype(BF16)
    low = (wide - high.astype(F32)).astype(BF16)
    return high, low


def one(left, right, dims):
    return lax.dot_general(left, right, dims, preferred_element_type=F32)


def product(left, right, dims):
    if not isinstance(left, tuple):
        return one(left, right[0], dims) + one(left, right[1], dims)
    if not isinstance(right, tuple):
        return one(left[0], right, dims) + one(left[1], right, dims)
    return one(left[0], right[0], dims) + (one(left[0], right[1], dims) + one(left[1], right[0], dims))


def feature(raw):
    wide = raw.astype(F32)
    return jnp.where(wide > 0, wide + 1.0, jnp.exp(jnp.minimum(wide, 0.0)))


def slope(raw):
    wide = raw.astype(F32)
    return jnp.where(wide > 0, 1.0, jnp.exp(jnp.minimum(wide, 0.0)))


def causal(size):
    row = lax.broadcasted_iota(jnp.int32, (size, size), 0)
    column = lax.broadcasted_iota(jnp.int32, (size, size), 1)
    return row >= column


def features_of(head):
    return slice(head * HD, head * HD + HD)


def local_kernel(at_ref, k_in, v_in, q_in, g_in, gain_in, k_ref, v_ref, q_ref, first_ref, g_ref, gain_ref, sems):
    pairs = ((k_in, k_ref), (v_in, v_ref), (g_in, g_ref), (gain_in, gain_ref), (q_in, q_ref))
    copies = [pltpu.make_async_copy(start, end, sems.at[place]) for place, (start, end) in enumerate(pairs)]
    for copy in copies:
        copy.start()
    copies[0].wait()
    copies[1].wait()
    for head in range(HEADS):
        part = features_of(head)
        first_ref[head] = product(halves(feature(k_ref[:, part])), v_ref[:, part], TN)
    for copy in copies[2:]:
        copy.wait()
    for head in range(HEADS):
        first_ref[HEADS + head] = gain_ref[head : head + 1, :] * g_ref[:, features_of(head)].astype(F32)


def core_of(at_ref):
    return lax.rem(at_ref[0], 2)


def total_kernel(pieces_ref, copy_ref, out_ref):
    copy_ref[...] = pieces_ref[...]
    total = pieces_ref[:, 0]
    for place in range(1, pieces_ref.shape[1]):
        total = total + pieces_ref[:, place]
    out_ref[...] = total


def total_and_pack_kernel(pieces_ref, prefix_ref, grad_ref, third_ref, out_ref):
    x_size, place_size, rows = pieces_ref.shape[:3]
    each = HD // rows
    for x in range(x_size):
        total = pieces_ref[x, 0]
        for place in range(1, place_size):
            total = total + pieces_ref[x, place]
        out_ref[x] = total
        for place in range(place_size):
            member = x * place_size + place
            third_ref[member // each, pl.ds(member % each * rows, rows), :] = pieces_ref[x, place]
    third_ref[HEADS : 2 * HEADS] = prefix_ref[...]
    third_ref[2 * HEADS :] = grad_ref[...]


def slots(place_size):
    return (1, 0) + tuple(range(2, place_size))


def prefix_kernel(backward, steps, place_size, source, at_ref, pieces_ref, *refs):
    far_refs, out_ref = refs[:-1], refs[-1]
    x_size, rows = far_refs[0].shape[:2]
    each = HD // rows
    blocks = len(steps) + 1
    block = lax.rem(lax.div(at_ref[0], 2 * place_size), blocks)
    base = jnp.zeros((rows, HD), F32)
    for x in range(x_size)[:: -1 if backward else 1]:
        so_far = row = base
        for step, far_ref in zip(steps, far_refs):
            other = lax.rem(block + blocks - step, blocks)
            total = far_ref[x]
            row = row + total
            so_far = so_far + jnp.where(other > block if backward else other < block, total, 0.0)
        for place in range(place_size)[:: -1 if backward else 1]:
            slot = slots(place_size)[place]
            member = x * place_size + slot
            piece = pieces_ref[source, member // each, pl.ds(member % each * rows, rows), :]
            out_ref[x, slot] = so_far
            so_far = so_far + piece
            row = row + piece
        base = row


def scores_kernel(at_ref, q_ref, k_ref, v_ref, pieces_ref, first_ref, scores_ref, second_ref):
    mask = causal(q_ref.shape[0])
    late = core_of(at_ref) == 1
    second_ref[:HEADS] = pieces_ref[...]
    for head in range(HEADS):
        part = features_of(head)
        wide = feature(q_ref[:, part])
        query = halves(wide)
        key = halves(feature(k_ref[:, part]))
        scores = jnp.where(mask, product(query, key, NT), 0.0)
        scores_ref[head] = scores
        before = halves(jnp.where(late, first_ref[0, head], 0.0))
        second_ref[HEADS + head] = product(halves(scores), v_ref[:, part], NN) + product(query, before, NN)
        second_ref[2 * HEADS + head] = wide


def split_kernel(second_ref, high_ref, low_ref, high_t_ref, low_t_ref):
    for head in range(HEADS):
        wide = second_ref[:, 2 * HEADS + head].reshape(2 * HD, HD)
        high_ref[head], low_ref[head] = halves(wide)
        high_t_ref[head], low_t_ref[head] = halves(wide.T)


def forward_kernel(first_ref, second_ref, high_ref, low_ref, high_t_ref, low_t_ref, prefix_ref, grad0_ref, grad1_ref, chip_ref):
    for head in range(HEADS):
        rows = (2 * HD, HD)
        query = high_ref[head], low_ref[head]
        output = second_ref[:, HEADS + head].reshape(rows) + product(query, halves(prefix_ref[head]), NN)
        inverse = lax.rsqrt(jnp.mean(output * output, axis=-1, keepdims=True) + 1e-06)
        scaled = first_ref[:, HEADS + head].reshape(rows)
        shared = jnp.mean(scaled * output, axis=-1, keepdims=True)
        grad = inverse * (scaled - output * (inverse * inverse * shared))
        chip_ref[head] = product((high_t_ref[head], low_t_ref[head]), halves(grad), NN)
        grad0_ref[head] = grad[:HD]
        grad1_ref[head] = grad[HD:]


def inner_kernel(at_ref, *refs):
    q_ref, k_ref, v_ref, scores_ref, grad_ref, first_ref, second_ref, third_ref, dq_ref, dk_ref, dv_ref, other_ref = refs
    mask = causal(q_ref.shape[0])
    late = core_of(at_ref) == 1
    for head in range(HEADS):
        part = features_of(head)
        query = halves(feature(q_ref[:, part]))
        key = halves(feature(k_ref[:, part]))
        grad = halves(jnp.where(late, third_ref[0, 2 * HEADS + head], grad_ref[head]))
        prefix = halves(third_ref[0, HEADS + head] + jnp.where(late, first_ref[0, head], 0.0))
        grad_scores = halves(jnp.where(mask, product(grad, v_ref[:, part], NT), 0.0))
        dq_ref[:, part] = slope(q_ref[:, part]) * (product(grad_scores, key, NN) + product(grad, prefix, NT))
        dk_ref[:, part] = product(grad_scores, query, TN)
        dv_ref[:, part] = product(halves(scores_ref[head]), grad, TN)
        later = halves(second_ref[1, 2 * HEADS + head]), halves(third_ref[0, 2 * HEADS + head])
        other_ref[head] = product(*later, TN)


def backward_kernel(at_ref, k_ref, v_ref, near_dk_ref, near_dv_ref, other_ref, last_ref, dk_out, dv_out, dk_ref, dv_ref, sems):
    late = core_of(at_ref) == 1
    suffixes = [halves(last_ref[1, head] + jnp.where(late, 0.0, other_ref[head])) for head in range(HEADS)]
    copies = [pltpu.make_async_copy(dk_ref, dk_out, sems.at[0]), pltpu.make_async_copy(dv_ref, dv_out, sems.at[1])]
    for head in range(HEADS):
        part = features_of(head)
        raw = k_ref[:, part]
        dk_ref[:, part] = slope(raw) * (near_dk_ref[:, part] + product(v_ref[:, part], suffixes[head], NT))
    copies[0].start()
    for head in range(HEADS):
        part = features_of(head)
        dv_ref[:, part] = near_dv_ref[:, part] + product(halves(feature(k_ref[:, part])), suffixes[head], NN)
    copies[1].start()
    for copy in copies:
        copy.wait()


def call(kernel, outs, *operands, scalars=0, inputs=VMEM, outputs=VMEM, scratch=()):
    return pl.pallas_call(
        kernel,
        out_shape=[jax.ShapeDtypeStruct(shape, dtype) for shape, dtype in outs],
        in_specs=[SMEM] * scalars + [inputs] * (len(operands) - scalars),
        out_specs=[outputs] * len(outs),
        scratch_shapes=scratch,
        compiler_params=pltpu.CompilerParams(vmem_limit_bytes=8 << 20),
    )(*operands)


def body(query, key, value, gain, grad_out):
    tokens = query.shape[0]
    at = lax.axis_index(SEQ).reshape(1)
    core = lax.axis_index("c")
    blocks, x_size, place_size = lax.axis_size("zb"), lax.axis_size("x"), lax.axis_size("zp")
    members = x_size * place_size
    piece = (HEADS * HD // members, HD)
    flat, near, far = (members,) + piece, (x_size, place_size) + piece, (x_size,) + piece
    state, three, wide = (HEADS, HD, HD), (3 * HEADS, HD, HD), (tokens, HEADS * HD)
    steps = sorted(range(1, blocks), key=lambda step: min(step, blocks - step))

    leading = sorted(range(place_size), key=lambda place: slots(place_size)[place])
    groups = [
        [((x * blocks + block) * place_size + place) * 2 + one_core for x in range(x_size) for place in leading]
        for block in range(blocks)
        for one_core in range(2)
    ]

    def within(pieces, shape):
        return lax.all_to_all(pieces.reshape(flat), SEQ, 0, 0, axis_index_groups=groups).reshape(shape)

    def to_blocks(total, source):
        ends = [(step, [(2 * block + source, 2 * ((block + step) % blocks) + 1 - source) for block in range(blocks)]) for step in steps]
        return [lax.ppermute(total, ("zb", "c"), pairs) for step, pairs in ends]

    def none(*shapes):
        return lambda *operands: tuple(jnp.zeros(shape, F32) for shape in shapes)

    def sums(backward, source, pieces, totals):
        kernel = functools.partial(prefix_kernel, backward, steps, place_size, source)
        return within(call(kernel, [(near, F32)], at, pieces, *totals, scalars=1)[0], state)

    given = (key, value, query, grad_out, gain.reshape(HEADS, HD))
    k, v, q, first = call(
        local_kernel,
        [(wide, BF16)] * 3 + [((2 * HEADS, HD, HD), F32)],
        at,
        *(pltpu.with_memory_space_constraint(array, pltpu.HBM) for array in given),
        scalars=1,
        inputs=HBM,
        scratch=[pltpu.VMEM(wide, BF16), pltpu.VMEM((HEADS, HD), F32), pltpu.SemaphoreType.DMA((5,))],
    )
    firsts = lax.all_gather(first, "c")

    def start(firsts):
        chip = firsts[0, :HEADS] + firsts[1, :HEADS]
        return tuple(call(total_kernel, [(near, F32), (far, F32)], within(chip, near)))

    pieces, total = lax.cond(core == 1, start, none(near, far), firsts)
    totals = to_blocks(total, 1)
    scores, second = call(scores_kernel, [(state, F32), (three, F32)], at, q, k, v, pieces.reshape(state), firsts, scalars=1)
    seconds = lax.all_gather(second, "c")
    tall, flat_t = ((HEADS, 2 * tokens, HD), BF16), ((HEADS, HD, 2 * tokens), BF16)
    queries = call(split_kernel, [tall, tall, flat_t, flat_t], seconds)

    def middle(firsts, seconds, queries, totals):
        prefix = sums(False, 1, seconds, totals)
        grad0, grad1, chip = call(forward_kernel, [(state, F32)] * 3, firsts, seconds, *queries, prefix)
        third, total = call(total_and_pack_kernel, [(three, F32), (far, F32)], within(chip, near), prefix, grad1)
        return third, total, grad0

    third, total, grad = lax.cond(core == 0, middle, none(three, far, state), firsts, seconds, queries, totals)
    totals = to_blocks(total, 0)
    thirds = lax.all_gather(third, "c")
    outs = [(wide, F32)] * 3 + [(state, F32)]
    dq, dk, dv, other = call(inner_kernel, outs, at, q, k, v, scores, grad, firsts, seconds, thirds, scalars=1)

    def end(thirds, totals):
        return (sums(True, 0, thirds, totals),)

    (last,) = lax.cond(core == 1, end, none(state), thirds, totals)
    lasts = lax.all_gather(last, "c")
    dk, dv = call(
        backward_kernel,
        [(wide, F32)] * 2,
        *(at, k, v, dk, dv, other, lasts),
        scalars=1,
        outputs=HBM,
        scratch=[pltpu.VMEM(wide, F32)] * 2 + [pltpu.SemaphoreType.DMA((2,))],
    )
    return dq, dk, dv


def over(devices):
    mesh = Mesh(devices, ("x", "zb", "zp", "c", "h"))
    placed = P(("x", "zb", "zp", "c"), "h")
    return jax.shard_map(
        body,
        mesh=mesh,
        in_specs=(placed, placed, placed, P("h"), placed),
        out_specs=(placed, placed, placed),
        check_vma=False,
    )


def solution(mesh):
    seq, head = mesh.devices.shape
    return over(mesh.devices.reshape(4, 4, seq // 32, 2, head))
```
